256 devices in a mesh: dp: 8 (over y, x_lo), seq: 32 (over z, x_hi, core).
Axes of the slice: x: 4 (x_hi: 2, x_lo: 2; x = x_hi * 2 + x_lo), y: 4, z: 8, core: 2. Of those that a mesh axis runs over, the one named last changes fastest.
Arguments:
- context_ids: int32 [262144], P(('dp', 'seq')), parts along dimension 0, may hold values from 0 to 255
- embed_table: bfloat16 [256, 1024], replicated, may hold values from -6 to 6
- latent_states: bfloat16 [2048, 1024], P(('dp', 'seq')), parts along dimension 0, may hold values from -3 to 3
- limits: int32 [2048], P('dp'), parts along dimension 0, may hold values from 16385 to 32768, as said below
- cross_q: bfloat16 [1024, 1024], replicated
- cross_kv: bfloat16 [1024, 2048], replicated, may hold values from -0.1875 to 0.1875
- cross_o: bfloat16 [1024, 1024], replicated, may hold values from -0.75 to 0.75
- attn_gain: float32 [1024], replicated, may hold values from 0.1 to 1.9
- self_qkv: bfloat16 [1024, 3072], P(None, 'seq')
- self_o: bfloat16 [1024, 1024], P(None, 'seq'), may hold values from -0.1875 to 0.1875
- mlp_gain: float32 [1024], replicated, may hold values from 0.1 to 1.9
- mlp_up: bfloat16 [1024, 4096], P(None, 'seq'), may hold values from -0.1875 to 0.1875
- mlp_down: bfloat16 [4096, 1024], P('seq'), may hold values from -0.1875 to 0.1875
Outputs:
- updated_latents: float32 [2048, 1024], P(('dp', 'seq')), parts along dimension 0
The draws below stay inside these ranges and needn't reach their ends.
There are 8 independent parts, one for each index of `dp`. The reference program is written for one: setup_inputs(seed, part) draws one part's arguments, and reference() takes and returns one part's arrays. A program takes and returns all parts, laid end to end along the dimension named above; an argument that names none is the same for every part. Nothing has to cross between parts.
Inputs may be any that keep to these rules, and one draw needn't show every extreme that they name: `limits`: non-decreasing along the latent rows; the first row sees 32768 // 2 + 1 positions and the last row all 32768.
All inputs are finite; a program needn't handle non-finite values.
Results may differ from the reference program's by a relative error of at most 0.02.
The reference program's roundings to bfloat16 on the way count: a program that leaves them out, or rounds other values in their place, can miss the bound.
Values may be sent and summed in bfloat16 or wider, within the bound.
A program may use at most 128 MiB of HBM per device.

```python
import math
import jax
import jax.numpy as jnp
from jax import lax

D = 1024
HEADS = 16
FF = 4096
VOCAB = 256
CTX_DEV = 1024
REGION = 64
HEAD = 64
CONTEXT = 32768
LAT = 256
N_SEQ = 32


def draw_context_ids(key, part):
    key = jax.random.fold_in(key, 5)
    region_key, first_key, second_key = jax.random.split(key, 3)
    region_count = CONTEXT // REGION
    offsets = jax.random.randint(region_key, (region_count,), 0, VOCAB)
    first = jax.random.randint(first_key, (CONTEXT,), 0, 32)
    second = jax.random.randint(second_key, (CONTEXT,), 0, 32)
    spread = first * second // 32
    region_of = jnp.arange(CONTEXT, dtype=jnp.int32) // REGION
    return ((offsets[region_of] + spread) % VOCAB).astype(jnp.int32)


def draw_limits(key, part):
    key = jax.random.fold_in(key, 11)
    half_context = CONTEXT // 2
    raw_limits = jax.random.randint(key, (LAT,), half_context + 1, CONTEXT + 1)
    ordered = jnp.sort(raw_limits)
    ordered = ordered.at[0].set(half_context + 1).at[LAT - 1].set(CONTEXT)
    return ordered.astype(jnp.int32)


def draw_cross_q(key, part):
    key = jax.random.fold_in(key, 23)
    matrix = jax.random.normal(key, (D, D), jnp.float32) * D ** (-0.5) * 3.0
    return matrix.astype(jnp.bfloat16)


def draw_self_qkv(key, part):
    key = jax.random.fold_in(key, 37)
    matrix = jax.random.normal(key, (D, 3 * D), jnp.float32) * D ** (-0.5)
    return matrix.astype(jnp.bfloat16)


def strengthened(drawn, key, source, target, parts, factor):
    def block_of(position):
        return (jnp.arange(drawn.shape[position]) // (drawn.shape[position] // parts)).reshape((-1,) + (1,) * (drawn.ndim - 1 - position))

    one_side = jax.random.permutation(key, parts)[block_of(target)]
    second = (block_of(target) + parts // 2) % parts
    return jnp.where((block_of(source) == one_side) | (block_of(source) == second), factor * drawn, drawn)


def block_scale(stream_key, shape, cuts, low, top_value):
    def one(axis_at, blocks):
        heights = jax.random.uniform(jax.random.fold_in(jax.random.fold_in(stream_key, 6), axis_at), (blocks,), jnp.float32, low / len(cuts), top_value / len(cuts))
        return jnp.repeat(jnp.exp(heights), shape[axis_at] // blocks).reshape((-1,) + (1,) * (len(shape) - axis_at - 1))

    level = one(*cuts[0])
    for cut in cuts[1:]:
        level = level * one(*cut)
    return level


def noise(rng, dims, width, bound, cuts=(), kind=jnp.bfloat16):
    entries = jax.random.normal(rng, dims, jnp.float32) * width
    if len(cuts) > 0:
        entries = block_scale(rng, dims, cuts, -0.22, 0.18) * entries
    return jnp.clip(entries, min=-bound, max=bound).astype(kind)


def bell_draw_with(own_key, extent, scale, limit, cuts, heavy, held_as=jnp.bfloat16):
    entries = scale * jax.random.normal(own_key, extent, jnp.float32)
    if cuts:
        entries = entries * block_scale(own_key, extent, cuts, -0.22, 0.18)
    return jnp.clip(strengthened(entries, jax.random.fold_in(own_key, 3), *heavy), -limit, limit).astype(held_as)


def setup_inputs(seed: int = 0, part: int = 0) -> dict:
    key_of = jax.random.split(jax.random.key(seed), 14)
    part_keys = jax.random.split(jax.random.fold_in(key_of[13], part), 14)
    return {
        "context_ids": draw_context_ids(jax.random.fold_in(jax.random.fold_in(key_of[13], part), 71), part),
        "embed_table": noise(key_of[1], (VOCAB, D), 1.0, 6.0),
        "latent_states": noise(part_keys[2], (LAT, D), 0.5, 3.0, ((0, 32),)),
        "limits": draw_limits(jax.random.fold_in(jax.random.fold_in(key_of[13], part), 71), part),
        "cross_q": draw_cross_q(jax.random.fold_in(key_of[13], 71), part),
        "cross_kv": noise(key_of[5], (D, 2 * D), D ** -0.5, 0.1875),
        "cross_o": noise(key_of[6], (D, D), HEAD ** -0.5, 0.75),
        "attn_gain": jnp.clip(1.0 + 0.18 * jax.random.normal(key_of[7], (D,), jnp.float32), 0.1, 1.9),
        "self_qkv": draw_self_qkv(jax.random.fold_in(key_of[13], 71), part),
        "self_o": noise(key_of[9], (D, D), D ** -0.5, 0.1875, ((1, 32),)),
        "mlp_gain": jnp.clip(1.0 + 0.18 * jax.random.normal(key_of[10], (D,), jnp.float32), 0.1, 1.9),
        "mlp_up": noise(key_of[11], (D, FF), D ** -0.5, 0.1875, ((1, 32),)),
        "mlp_down": bell_draw_with(key_of[12], (FF, D), FF ** -0.5, 0.1875, ((0, 32),), (0, 1, 32, 2.75)),
    }


def rms_scale(states, gain):
    mean_sq = lax.optimization_barrier(jnp.mean(states * states, axis=-1, keepdims=True))
    return states * lax.rsqrt(mean_sq + 1e-05) * gain

def rotate_rows(rows_in, positions, head_size):
    half_size = head_size // 2
    period_list = [int(4.0 * 16384.0 ** (freq_index / (half_size - 1))) for freq_index in range(half_size)]
    periods = jnp.array(period_list, dtype=jnp.int32)
    factors = jnp.array([2.0 * math.pi / period for period in period_list], dtype=jnp.float32)
    phase = (positions[:, None] % periods[None, :]).astype(jnp.float32) * factors[None, :]
    cosines = jnp.cos(phase)[:, None, :]
    sine_values = jnp.sin(phase)[:, None, :]
    count_rows = rows_in.shape[0]
    parted = rows_in.reshape(count_rows, -1, head_size)
    first_half = parted[..., :half_size]
    second_half = parted[..., half_size:]
    turned = jnp.concatenate([first_half * cosines - second_half * sine_values, second_half * cosines + first_half * sine_values], axis=-1)
    return turned.reshape(count_rows, -1).astype(jnp.bfloat16)

def reference(context_ids, embed_table, latent_states, limits, cross_q, cross_kv, cross_o, attn_gain, self_qkv, self_o, mlp_gain, mlp_up, mlp_down):
    head_size = D // HEADS
    score_scale = 1.0 / math.sqrt(head_size)
    embedded = embed_table[context_ids]
    key_value = jnp.dot(embedded, cross_kv, preferred_element_type=jnp.float32)
    context_pos = jnp.arange(CONTEXT, dtype=jnp.int32)
    rotated_keys = lax.optimization_barrier(rotate_rows(key_value[:, :D], context_pos, head_size))
    rounded_values = lax.optimization_barrier(key_value[:, D:].astype(jnp.bfloat16))
    context_keys = rotated_keys.astype(jnp.float32).reshape(N_SEQ, CTX_DEV, HEADS, head_size)
    context_values = rounded_values.astype(jnp.float32).reshape(N_SEQ, CTX_DEV, HEADS, head_size)
    queries = jnp.dot(latent_states, cross_q, preferred_element_type=jnp.float32)
    rotated_queries = lax.optimization_barrier(rotate_rows(queries, limits - 1, head_size))
    query_rows = rotated_queries.astype(jnp.float32).reshape(LAT, HEADS, head_size)
    block_starts = jnp.arange(N_SEQ, dtype=jnp.int32) * CTX_DEV

    def block_terms(inputs):
        key_block, value_block, first_row = inputs
        scores = jnp.einsum('qhd,khd->hqk', query_rows, key_block) * score_scale
        positions = first_row + jnp.arange(CTX_DEV, dtype=jnp.int32)
        visible = (positions[None, :] < limits[:, None])[None]
        masked = jnp.where(visible, scores, -1e+30)
        row_peak = lax.optimization_barrier(jnp.max(masked, axis=2))
        weights = jnp.where(visible, jnp.exp(masked - row_peak[:, :, None]), 0.0).astype(jnp.bfloat16)
        weights = lax.optimization_barrier(weights).astype(jnp.float32)
        row_total = lax.optimization_barrier(jnp.sum(weights, axis=2))
        numerators = jnp.einsum('hqk,khd->qhd', weights, value_block)
        return (numerators, row_peak.T, row_total.T)
    numerators, block_peak, block_total = lax.map(block_terms, (context_keys, context_values, block_starts))
    row_top = lax.optimization_barrier(jnp.max(block_peak, axis=0))
    rescale = jnp.exp(block_peak - row_top[None])
    summed = lax.optimization_barrier(jnp.sum(numerators * rescale[..., None], axis=0))
    totals = lax.optimization_barrier(jnp.sum(block_total * rescale, axis=0))
    cross_mix = (summed / totals[..., None]).reshape(LAT, D).astype(jnp.bfloat16)
    latents = latent_states.astype(jnp.float32) + jnp.dot(cross_mix, cross_o, preferred_element_type=jnp.float32)
    normed = rms_scale(latents, attn_gain).astype(jnp.bfloat16)
    projected = jnp.dot(normed, self_qkv, preferred_element_type=jnp.float32).astype(jnp.bfloat16)
    projected = lax.optimization_barrier(projected).astype(jnp.float32)
    self_queries = projected[:, :D].reshape(LAT, HEADS, head_size)
    self_keys = projected[:, D:2 * D].reshape(LAT, HEADS, head_size)
    self_values = projected[:, 2 * D:].reshape(LAT, HEADS, head_size)
    scores = jnp.einsum('qhd,khd->hqk', self_queries, self_keys, precision=lax.Precision.HIGHEST) * score_scale
    rows = jnp.arange(LAT, dtype=jnp.int32)
    causal = (rows[None, :] <= rows[:, None])[None]
    masked = jnp.where(causal, scores, -1e+30)
    row_peak = lax.optimization_barrier(jnp.max(masked, axis=2, keepdims=True))
    weights = jnp.where(causal, jnp.exp(masked - row_peak), 0.0)
    mixed = jnp.einsum('hqk,khd->qhd', weights, self_values, precision=lax.Precision.HIGHEST)
    mixed = mixed / lax.optimization_barrier(jnp.sum(weights, axis=2)).T[..., None]
    self_mix = mixed.reshape(LAT, D).astype(jnp.bfloat16)
    attended = latents + jnp.dot(self_mix, self_o, preferred_element_type=jnp.float32)
    normed_mlp = rms_scale(attended, mlp_gain).astype(jnp.bfloat16)
    hidden = jax.nn.gelu(jnp.dot(normed_mlp, mlp_up, preferred_element_type=jnp.float32), approximate=True).astype(jnp.bfloat16)
    return attended + jnp.dot(hidden, mlp_down, preferred_element_type=jnp.float32)
```

```python
import math

import jax
import jax.numpy as jnp
import numpy as np
from jax import lax
from jax.experimental import pallas as pl
from jax.experimental.pallas import tpu as pltpu
from jax.sharding import PartitionSpec as P

F32 = jnp.float32
BF16 = jnp.bfloat16
MESH = pl.DeviceIdType.MESH
LOW = -1e30


def trig_tables():
    periods = np.array([int(4.0 * 16384.0 ** (f / 31)) for f in range(32)], np.int64)

    def angles(positions):
        return 2.0 * np.pi * (positions[None, :] % periods[:, None]) / periods[:, None]

    base = angles(np.arange(1024))
    base = np.concatenate([np.cos(base), np.sin(base)]).astype(np.float32)
    start = angles(np.arange(32) * 1024)
    start = np.concatenate([np.cos(start), np.sin(start)]).astype(np.float32)
    start = np.pad(start, ((0, 0), (0, 96)))
    by_lane = np.tile(periods, 4).astype(np.float64)
    lanes = np.zeros((8, 128), np.float32)
    lanes[0], lanes[1], lanes[2] = by_lane, 1.0 / by_lane, 2.0 * np.pi / by_lane
    return base, start, lanes


def dot(left, right):
    return lax.dot_general(left, right, (((1,), (0,)), ((), ())), preferred_element_type=F32)


def dot_nt(left, right):
    return lax.dot_general(left, right, (((1,), (1,)), ((), ())), preferred_element_type=F32)


def iota(shape, axis):
    return lax.broadcasted_iota(jnp.int32, shape, axis)


def rms_scale(states, gain):
    mean_sq = jnp.mean(states * states, axis=-1, keepdims=True)
    return states * lax.rsqrt(mean_sq + 1e-05) * gain


def kernel(
    ids_ref, states_ref, limits_ref, attn_gain, mlp_gain, qkv_ref, selfo_ref, start_ref, lanes_ref,
    base_hbm, embed_hbm, crossq_hbm, crosskv_hbm, crosso_hbm, up_hbm, down_hbm,
    out_ref,
    crossq, embed, ck, cv, base, crosso, updown_up, updown_dn,
    lim_nat, lim_perm, qsrc, qbuf, ids_all, stpack, strecv, wt, wqkv, selfo,
    acc, peak, packs, comb, mixsrc, mixrecv, mixf, lat, kvall, mix2all, atts, part, precv,
    loc, ss, rs, rs_up, rs_dn, rs_w, rs_kv,
):
    me = lax.axis_index("seq")
    dp = lax.axis_index("dp")
    core = lax.rem(me, 2)
    chip = me // 2
    x = lax.rem(chip, 2)
    z = chip // 2
    quad = lax.rem(me, 4)
    sib = me + 1 - 2 * core
    across = me + 2 - 4 * x
    diagonal = sib + 2 - 4 * x
    dp_pair = dp + 1 - 2 * lax.rem(dp, 2)
    quad_x = quad + 2 - 4 * x

    def same_core(i):
        return lax.rem(chip + i, 16)

    def remote(src, dst, send, recv, seq, part_of=None):
        where = {"seq": seq} if part_of is None else {"dp": part_of, "seq": seq}
        return pltpu.make_async_remote_copy(
            src_ref=src, dst_ref=dst, send_sem=send, recv_sem=recv, device_id=where, device_id_type=MESH
        )

    def over(count, body):
        lax.fori_loop(1, count, lambda i, carry: (body(i), carry)[1], 0)

    barrier = pltpu.get_barrier_semaphore()

    def greet(seq, part_of=None):
        where = {"seq": seq} if part_of is None else {"dp": part_of, "seq": seq}
        pl.semaphore_signal(barrier, inc=1, device_id=where, device_id_type=MESH)

    over(16, lambda i: greet(2 * same_core(i) + core))
    greet(sib)
    greet(diagonal)
    greet(across, dp_pair)

    columns = pl.multiple_of(128 * z, 128)
    local = [
        pltpu.make_async_copy(crossq_hbm, crossq, loc.at[0]),
        pltpu.make_async_copy(embed_hbm, embed, loc.at[1]),
        pltpu.make_async_copy(crosskv_hbm.at[:, pl.ds(columns, 128)], ck, loc.at[2]),
        pltpu.make_async_copy(crosskv_hbm.at[:, pl.ds(columns + 1024, 128)], cv, loc.at[3]),
        pltpu.make_async_copy(base_hbm, base, loc.at[4]),
        pltpu.make_async_copy(up_hbm, updown_up.at[quad], loc.at[5]),
        pltpu.make_async_copy(down_hbm, updown_dn.at[quad], loc.at[6]),
        pltpu.make_async_copy(crosso_hbm, crosso, loc.at[7]),
    ]
    for copy in local:
        copy.start()

    lim_nat[...] = jnp.broadcast_to(limits_ref[...].astype(F32), (128, 256)).T
    for c_of in range(2):
        for x_of in range(2):
            for z_of in range(8):
                slot = ((c_of * 2 + x_of) * 8 + z_of) * 8
                row = (z_of * 4 + x_of * 2 + c_of) * 8
                lim_perm[slot : slot + 8, :] = lim_nat[row : row + 8, :]

    local[0].wait()
    raw = dot(states_ref[...], crossq[...])
    period, inverse, factor = lanes_ref[0:1, :], lanes_ref[1:2, :], lanes_ref[2:3, :]
    position = lim_nat[pl.ds(pl.multiple_of(8 * me, 8), 8), :] - 1.0
    phase = position - jnp.floor(position * inverse) * period
    phase = jnp.where(phase < 0.0, phase + period, phase)
    phase = jnp.where(phase >= period, phase - period, phase) * factor
    lane8 = iota((8, 128), 1)
    first = lax.rem(lane8, 64) < 32
    cosines = jnp.cos(phase)
    sines = jnp.sin(phase)
    sines = jnp.where(first, -sines, sines)
    for p in range(8):
        tile = raw[:, 128 * p : 128 * p + 128]
        swapped = jnp.where(first, pltpu.roll(tile, 96, 1), pltpu.roll(tile, 32, 1))
        qsrc[p] = (tile * cosines + swapped * sines).astype(BF16).astype(F32) * 0.125
    qbuf[core, x * 8 + z] = qsrc[z]
    ids_all[chip] = ids_ref[...]
    packed = states_ref[...].astype(F32)
    packed = jnp.concatenate([packed[:, :512], packed[:, 512:]], axis=0).astype(BF16)
    stpack[...] = packed
    strecv[z] = packed

    pl.semaphore_wait(barrier, 18)

    def send_ids(i):
        k = same_core(i)
        remote(ids_ref, ids_all.at[chip], ss.at[0], rs.at[0], 2 * k + core).start()
        remote(qsrc.at[k // 2], qbuf.at[core, x * 8 + z], ss.at[1], rs.at[1], 2 * k + core).start()

    over(16, send_ids)

    def ring(i):
        return lax.rem(me + 4 * i, 32)

    over(8, lambda i: remote(stpack, strecv.at[z], ss.at[2], rs.at[2], ring(i)).start())
    own_up = [
        remote(up_hbm, updown_up.at[quad], ss.at[3], rs_up.at[quad], sib),
        remote(down_hbm, updown_dn.at[quad], ss.at[4], rs_dn.at[quad], sib),
        remote(up_hbm, updown_up.at[quad], ss.at[5], rs_up.at[quad], across, dp_pair),
        remote(down_hbm, updown_dn.at[quad], ss.at[6], rs_dn.at[quad], across, dp_pair),
    ]
    for copy in own_up:
        copy.start()

    eye = (iota((128, 128), 0) == iota((128, 128), 1)).astype(F32).astype(BF16)
    both = jnp.concatenate([qkv_ref[...], selfo_ref[...]], axis=1)
    wt[...] = dot_nt(eye, both).astype(BF16).reshape(4, 32, 1024)
    selfo[chip, core] = wt[3]

    def unit_copies(i, x_of):
        unit = 3 * me + i
        index = 4 * (unit // 32) + lax.rem(unit, 4)
        target = 4 * (lax.rem(unit, 32) // 4) + 2 * x_of + core
        away = remote(wt.at[i], wqkv.at[index], ss.at[7 + 2 * i + x_of], rs_w.at[index], target)
        here = pltpu.make_async_copy(wt.at[i], wqkv.at[index], rs_w.at[index])
        return target, away, here

    for i in range(3):
        for x_of in range(2):
            target, away, here = unit_copies(i, x_of)
            pl.when(target != me)(away.start)
            pl.when(target == me)(here.start)

    over(
        16,
        lambda i: remote(
            wt.at[3], selfo.at[chip, core], ss.at[13], rs.at[3], 2 * same_core(i) + core
        ).start(),
    )

    local[1].wait()
    local[2].wait()
    local[3].wait()
    local[4].wait()
    key_rows = dot(embed[...], ck[...]).T
    key_rows = jnp.where(x == 0, key_rows[0:64], key_rows[64:128])
    value_rows = dot(embed[...], cv[...]).T
    value_rows = jnp.where(x == 0, value_rows[0:64], value_rows[64:128])
    key_top = key_rows.astype(BF16)
    key_rest = (key_rows - key_top.astype(F32)).astype(BF16)
    table = jnp.concatenate([key_top, key_rest, value_rows.astype(BF16)], axis=0)

    def wait_in(buf, sem):
        pltpu.make_async_copy(buf, buf, sem).wait()

    wait_in(ids_all.at[pl.ds(0, 15)], rs.at[0])
    wait_in(qbuf.at[core, pl.ds(0, 15)], rs.at[1])
    forward_q = remote(qbuf.at[core], qbuf.at[core], ss.at[14], rs.at[4], sib)
    forward_q.start()
    wait_in(qbuf.at[1 - core], rs.at[4])
    lane256 = iota((256, 128), 1)
    queries = jnp.where(lane256 // 64 == x, qbuf[...].reshape(256, 128), 0.0).astype(BF16)
    acc[...] = jnp.zeros((256, 128), F32)
    peak[...] = jnp.full((256, 128), LOW, F32)

    def context_block(j, masked):
        block = 2 * j + core
        onehot = (iota((256, 1024), 0) == ids_all[j]).astype(F32).astype(BF16)
        rows = dot(table, onehot)
        keys = rows[0:64] + rows[64:128]
        here = jnp.where(iota((64, 128), 1) == block, start_ref[...], 0.0)
        here = jnp.sum(here, axis=1, keepdims=True)
        cos_a, sin_a, cos_b, sin_b = here[0:32], here[32:64], base[0:32, :], base[32:64, :]
        cos = cos_a * cos_b - sin_a * sin_b
        sin = sin_a * cos_b + cos_a * sin_b
        one, two = keys[0:32], keys[32:64]
        turned = jnp.concatenate([one * cos - two * sin, two * cos + one * sin], axis=0)
        turned = turned.astype(BF16)
        scores = dot(queries, jnp.concatenate([turned, turned], axis=0))
        if masked:
            place = (block * 1024 + iota((1, 1024), 1)).astype(F32)
            scores = jnp.where(place < lim_perm[:, 0:1], scores, LOW)
        top = jnp.max(scores, axis=1, keepdims=True)
        weights = jnp.exp(scores - top).astype(BF16)
        values = jnp.concatenate([rows[128:192].astype(BF16), jnp.ones((64, 1024), BF16)], axis=0)
        terms = dot_nt(weights, values)
        old = peak[...]
        new = jnp.maximum(old, top)
        acc[...] = acc[...] * jnp.exp(old - new) + terms * jnp.exp(top - new)
        peak[...] = new

    lax.fori_loop(0, 8, lambda j, carry: (context_block(j, False), carry)[1], 0)
    lax.fori_loop(8, 16, lambda j, carry: (context_block(j, True), carry)[1], 0)

    packs[...] = jnp.where(lane256 == 127, peak[...], acc[...]).reshape(2, 128, 128)
    swap = remote(packs.at[1 - core], comb, ss.at[15], rs.at[5], sib)
    swap.start()

    wait_in(updown_up.at[quad_x], rs_up.at[quad_x])
    wait_in(updown_dn.at[quad_x], rs_dn.at[quad_x])
    forwards = [
        remote(updown_up.at[quad_x], updown_up.at[quad_x], ss.at[16], rs_up.at[quad_x], sib),
        remote(updown_dn.at[quad_x], updown_dn.at[quad_x], ss.at[17], rs_dn.at[quad_x], sib),
    ]
    for copy in forwards:
        copy.start()

    def unit_core(index):
        unit = 32 * (index // 4) + 4 * z + index % 4
        return lax.rem(unit // 3, 2)

    def unit_forward(index):
        return remote(wqkv.at[index], wqkv.at[index], ss.at[18 + index], rs_w.at[index], sib)

    def pass_unit(index):
        wait_in(wqkv.at[index], rs_w.at[index])
        unit_forward(index).start()

    for index in range(12):
        pl.when(unit_core(index) == core)(lambda index=index: pass_unit(index))

    wait_in(comb, rs.at[5])
    mine, theirs = packs[core], comb[...]
    peak_a, peak_b = mine[:, 127:128], theirs[:, 127:128]
    top = jnp.maximum(peak_a, peak_b)
    both = mine * jnp.exp(peak_a - top) + theirs * jnp.exp(peak_b - top)
    mixed = both / both[:, 64:65]
    lane32 = iota((32, 128), 1)
    for x_of in range(2):
        low, high = mixed[64 * x_of : 64 * x_of + 32], mixed[64 * x_of + 32 : 64 * x_of + 64]
        mixsrc[x_of] = jnp.where(lane32 < 64, low, pltpu.roll(high, 64, 1)).astype(BF16)
    mixrecv[chip] = mixsrc[x]

    def send_mix(i):
        k = same_core(i)
        remote(mixsrc.at[lax.rem(k, 2)], mixrecv.at[chip], ss.at[30], rs.at[6], 2 * k + core).start()

    over(16, send_mix)

    wait_in(selfo.at[pl.ds(0, 15), 0], rs.at[3])
    forward_o = remote(selfo.at[:, core], selfo.at[:, core], ss.at[31], rs.at[7], sib)
    forward_o.start()

    wait_in(strecv.at[pl.ds(0, 7)], rs.at[2])
    for z_of in range(8):
        rows = strecv[z_of].astype(F32)
        lat[8 * z_of : 8 * z_of + 8, :] = jnp.concatenate([rows[0:8], rows[8:16]], axis=1)
    for index in range(12):
        pl.when(unit_core(index) != core)(
            lambda index=index: wait_in(wqkv.at[index], rs_w.at[index])
        )
    local[7].wait()
    wait_in(mixrecv.at[pl.ds(0, 15)], rs.at[6])
    for p in range(8):
        even, odd = mixrecv[2 * p].astype(F32), mixrecv[2 * p + 1].astype(F32)
        above = jnp.where(lane32 < 64, even, pltpu.roll(odd, 64, 1))
        below = jnp.where(lane32 < 64, pltpu.roll(even, 64, 1), odd)
        mixf[:, 128 * p : 128 * p + 128] = jnp.concatenate([above, below], axis=0).astype(BF16)
    latents = lat[...] + dot(mixf[...], crosso[...])
    normed = rms_scale(latents, attn_gain[...]).astype(BF16)
    lat[...] = latents

    projected = dot_nt(normed, wqkv[...].reshape(384, 1024)).astype(BF16)
    kvall[quad] = projected[:, 128:384]
    kv_copies = [
        remote(kvall.at[quad], kvall.at[quad], ss.at[32 + n], rs_kv.at[quad], seq)
        for n, seq in enumerate((sib, across, diagonal))
    ]
    for copy in kv_copies:
        copy.start()
    for other in (1, 2, 3):
        slot = lax.rem(quad + other, 4)
        wait_in(kvall.at[slot], rs_kv.at[slot])
    lane64 = iota((64, 128), 1)
    keys = kvall[:, :, 0:128].reshape(256, 128)
    values = kvall[:, :, 128:256].reshape(256, 128)
    key_lane = iota((64, 256), 1)
    key_row = 32 * (lax.rem(key_lane, 64) // 8) + 8 * (key_lane // 64) + lax.rem(key_lane, 8)
    query_at = iota((64, 256), 0)
    query_row = 32 * (query_at // 8) + 8 * quad + lax.rem(query_at, 8)
    causal = key_row <= query_row
    heads = []
    for head in range(2):
        only = jnp.where(lane64 // 64 == head, projected[:, 0:128].astype(F32), 0.0).astype(BF16)
        scores = jnp.where(causal, dot_nt(only, keys) * 0.125, LOW)
        weights = jnp.exp(scores - jnp.max(scores, axis=1, keepdims=True))
        total = jnp.sum(weights, axis=1, keepdims=True)
        coarse = weights.astype(BF16)
        fine = (weights - coarse.astype(F32)).astype(BF16)
        heads.append((dot(coarse, values) + dot(fine, values)) / total)
    mix2all[z] = jnp.where(lane64 < 64, heads[0], heads[1]).astype(BF16)
    over(8, lambda i: remote(mix2all.at[z], mix2all.at[z], ss.at[35], rs.at[8], ring(i)).start())
    wait_in(selfo.at[:, 1 - core], rs.at[7])
    wait_in(mix2all.at[pl.ds(0, 7)], rs.at[8])
    mix2 = jnp.concatenate([mix2all[k] for k in range(8)], axis=1)
    attended = lat[...] + dot_nt(mix2, selfo[...].reshape(1024, 1024))
    atts[...] = attended.reshape(8, 8, 1024)
    normed = rms_scale(attended, mlp_gain[...]).astype(BF16)

    local[5].wait()
    local[6].wait()
    for slot in (quad + 1 - 2 * core, quad_x + 1 - 2 * core):
        wait_in(updown_up.at[slot], rs_up.at[slot])
        wait_in(updown_dn.at[slot], rs_dn.at[slot])
    hidden = []
    for half in range(2):
        ups = jnp.concatenate([updown_up[2 * half], updown_up[2 * half + 1]], axis=1)
        hidden.append(jax.nn.gelu(dot(normed, ups), approximate=True).astype(BF16))
    hidden = jnp.concatenate(hidden, axis=1)
    part[...] = dot(hidden, updown_dn[...].reshape(512, 1024)).reshape(8, 8, 1024)
    precv[z] = part[z]

    def send_part(i):
        seq = ring(i)
        remote(part.at[seq // 4], precv.at[z], ss.at[36], rs.at[9], seq).start()

    over(8, send_part)
    wait_in(precv.at[pl.ds(0, 7)], rs.at[9])
    total = atts[z]
    summed = precv[0]
    for k in range(1, 8):
        summed = summed + precv[k]
    out_ref[...] = total + summed

    def wait_out(buf, sem):
        pltpu.make_async_copy(buf, buf, sem).wait()

    wait_out(ids_all.at[pl.ds(0, 15)], ss.at[0])
    wait_out(qbuf.at[0, pl.ds(0, 15)], ss.at[1])
    wait_out(strecv.at[pl.ds(0, 7)], ss.at[2])
    for copy in own_up + forwards + kv_copies + [forward_q, swap, forward_o]:
        copy.wait_send()
    for i in range(3):
        for x_of in range(2):
            target, away, _ = unit_copies(i, x_of)
            pl.when(target != me)(away.wait_send)
    for index in range(12):
        pl.when(unit_core(index) == core)(lambda index=index: unit_forward(index).wait_send())
    wait_out(selfo.at[pl.ds(0, 15), 0], ss.at[13])
    wait_out(mixrecv.at[pl.ds(0, 15)], ss.at[30])
    wait_out(mix2all.at[pl.ds(0, 7)], ss.at[35])
    wait_out(precv.at[pl.ds(0, 7)], ss.at[36])


def on_device(
    context_ids, embed_table, latent_states, limits, cross_q, cross_kv, cross_o,
    attn_gain, self_qkv, self_o, mlp_gain, mlp_up, mlp_down,
):
    base, start, lanes = trig_tables()
    vmem = pl.BlockSpec(memory_space=pltpu.VMEM)
    anywhere = pl.BlockSpec(memory_space=pl.ANY)
    dma = pltpu.SemaphoreType.DMA
    return pl.pallas_call(
        kernel,
        out_shape=jax.ShapeDtypeStruct((8, 1024), F32),
        in_specs=[vmem] * 9 + [anywhere] * 7,
        out_specs=vmem,
        scratch_shapes=[
            pltpu.VMEM((1024, 1024), BF16),
            pltpu.VMEM((256, 1024), BF16),
            pltpu.VMEM((1024, 128), BF16),
            pltpu.VMEM((1024, 128), BF16),
            pltpu.VMEM((64, 1024), F32),
            pltpu.VMEM((1024, 1024), BF16),
            pltpu.VMEM((4, 1024, 128), BF16),
            pltpu.VMEM((4, 128, 1024), BF16),
            pltpu.VMEM((256, 128), F32),
            pltpu.VMEM((256, 128), F32),
            pltpu.VMEM((8, 8, 128), F32),
            pltpu.VMEM((2, 16, 8, 128), F32),
            pltpu.VMEM((16, 1, 1024), jnp.int32),
            pltpu.VMEM((16, 512), BF16),
            pltpu.VMEM((8, 16, 512), BF16),
            pltpu.VMEM((4, 32, 1024), BF16),
            pltpu.VMEM((12, 32, 1024), BF16),
            pltpu.VMEM((16, 2, 32, 1024), BF16),
            pltpu.VMEM((256, 128), F32),
            pltpu.VMEM((256, 128), F32),
            pltpu.VMEM((2, 128, 128), F32),
            pltpu.VMEM((128, 128), F32),
            pltpu.VMEM((2, 32, 128), BF16),
            pltpu.VMEM((16, 32, 128), BF16),
            pltpu.VMEM((64, 1024), BF16),
            pltpu.VMEM((64, 1024), F32),
            pltpu.VMEM((4, 64, 256), BF16),
            pltpu.VMEM((8, 64, 128), BF16),
            pltpu.VMEM((8, 8, 1024), F32),
            pltpu.VMEM((8, 8, 1024), F32),
            pltpu.VMEM((8, 8, 1024), F32),
            dma((8,)),
            dma((37,)),
            dma((10,)),
            dma((4,)),
            dma((4,)),
            dma((12,)),
            dma((4,)),
        ],
        compiler_params=pltpu.CompilerParams(
            collective_id=0, has_side_effects=True, vmem_limit_bytes=48 << 20
        ),
        name="ar_step",
    )(
        context_ids.reshape(1, -1), latent_states, limits.reshape(1, -1),
        attn_gain.reshape(1, -1), mlp_gain.reshape(1, -1), self_qkv, self_o,
        jnp.asarray(start), jnp.asarray(lanes), jnp.asarray(base),
        embed_table, cross_q, cross_kv, cross_o, mlp_up, mlp_down,
    )


def solution(mesh):
    placed = (
        P(("dp", "seq")),
        P(),
        P(("dp", "seq"), None),
        P("dp"),
        P(),
        P(),
        P(),
        P(),
        P(None, "seq"),
        P(None, "seq"),
        P(),
        P(None, "seq"),
        P("seq", None),
    )
    return jax.shard_map(
        on_device, mesh=mesh, in_specs=placed, out_specs=P(("dp", "seq"), None), check_vma=False
    )
```

```python
import math

import jax
import jax.numpy as jnp
import numpy as np
from jax import lax
from jax.experimental import pallas as pl
from jax.experimental.pallas import tpu as pltpu
from jax.sharding import PartitionSpec as P

F32 = jnp.float32
BF16 = jnp.bfloat16
MESH = pl.DeviceIdType.MESH
LOW = -1e30


def trig_tables():
    periods = np.array([int(4.0 * 16384.0 ** (f / 31)) for f in range(32)], np.int64)

    def angles(positions):
        return 2.0 * np.pi * (positions[None, :] % periods[:, None]) / periods[:, None]

    base = angles(np.arange(1024))
    base = np.concatenate([np.cos(base), np.sin(base)]).astype(np.float32)
    start = angles(np.arange(32) * 1024)
    start = np.concatenate([np.cos(start), np.sin(start)]).astype(np.float32)
    start = np.pad(start, ((0, 0), (0, 96)))
    by_lane = np.tile(periods, 4).astype(np.float64)
    lanes = np.zeros((8, 128), np.float32)
    lanes[0], lanes[1], lanes[2] = by_lane, 1.0 / by_lane, 2.0 * np.pi / by_lane
    return base, start, lanes


def dot(left, right):
    return lax.dot_general(left, right, (((1,), (0,)), ((), ())), preferred_element_type=F32)


def dot_nt(left, right):
    return lax.dot_general(left, right, (((1,), (1,)), ((), ())), preferred_element_type=F32)


def iota(shape, axis):
    return lax.broadcasted_iota(jnp.int32, shape, axis)


def rms_scale(states, gain):
    mean_sq = jnp.mean(states * states, axis=-1, keepdims=True)
    return states * lax.rsqrt(mean_sq + 1e-05) * gain


def kernel(
    ids_hbm, states_hbm, limits_hbm, attn_gain_hbm, mlp_gain_hbm, qkv_hbm, selfo_hbm, start_hbm, lanes_hbm,
    base_hbm, embed_hbm, crossq_hbm, crosskv_hbm, crosso_hbm, up_hbm, down_hbm,
    out_ref,
    ids_ref, states_ref, limits_ref, attn_gain, mlp_gain, start_ref, lanes_ref,
    crossq, embed, ck, cv, base, crosso, updown_up, updown_dn,
    lim_nat, lim_perm, qsrc, qbuf, ids_all, stpack, strecv, wt, wqkv, selfo,
    acc, peak, packs, comb, mixsrc, mixrecv, mixf, lat, kvall, mix2all, atts, part, precv,
    loc, ss, rs, rs_up, rs_dn, rs_w, rs_kv,
):
    me = lax.axis_index("seq")
    dp = lax.axis_index("dp")
    core = lax.rem(me, 2)
    chip = me // 2
    x = lax.rem(chip, 2)
    z = chip // 2
    quad = lax.rem(me, 4)
    sib = me + 1 - 2 * core
    across = me + 2 - 4 * x
    diagonal = sib + 2 - 4 * x
    dp_pair = dp + 1 - 2 * lax.rem(dp, 2)
    y = dp // 2
    carrier = lax.rem(z, 4) == y
    quad_x = quad + 2 - 4 * x

    def same_core(i):
        return lax.rem(chip + i, 16)

    def remote(src, dst, send, recv, seq, part_of=None):
        where = {"seq": seq} if part_of is None else {"dp": part_of, "seq": seq}
        return pltpu.make_async_remote_copy(
            src_ref=src, dst_ref=dst, send_sem=send, recv_sem=recv, device_id=where, device_id_type=MESH
        )

    def over(count, body):
        lax.fori_loop(1, count, lambda i, carry: (body(i), carry)[1], 0)

    barrier = pltpu.get_barrier_semaphore()

    def greet(seq, part_of=None):
        where = {"seq": seq} if part_of is None else {"dp": part_of, "seq": seq}
        pl.semaphore_signal(barrier, inc=1, device_id=where, device_id_type=MESH)

    over(16, lambda i: greet(2 * same_core(i) + core))
    greet(sib)
    greet(diagonal)
    greet(across, dp_pair)
    over(4, lambda i: greet(me, lax.rem(dp + 2 * i, 8)))

    columns = pl.multiple_of(128 * z, 128)
    local = [
        pltpu.make_async_copy(crossq_hbm, crossq, loc.at[0]),
        pltpu.make_async_copy(embed_hbm, embed, loc.at[1]),
        pltpu.make_async_copy(crosskv_hbm.at[:, pl.ds(columns, 128)], ck, loc.at[2]),
        pltpu.make_async_copy(crosskv_hbm.at[:, pl.ds(columns + 1024, 128)], cv, loc.at[3]),
        pltpu.make_async_copy(base_hbm, base, loc.at[4]),
        pltpu.make_async_copy(up_hbm, updown_up.at[quad], loc.at[5]),
        pltpu.make_async_copy(down_hbm, updown_dn.at[quad], loc.at[6]),
        pltpu.make_async_copy(crosso_hbm, crosso, loc.at[7]),
        pltpu.make_async_copy(ids_hbm, ids_ref, loc.at[8]),
        pltpu.make_async_copy(states_hbm, states_ref, loc.at[9]),
        pltpu.make_async_copy(limits_hbm, limits_ref, loc.at[10]),
        pltpu.make_async_copy(attn_gain_hbm, attn_gain, loc.at[11]),
        pltpu.make_async_copy(mlp_gain_hbm, mlp_gain, loc.at[12]),
        pltpu.make_async_copy(start_hbm, start_ref, loc.at[13]),
        pltpu.make_async_copy(lanes_hbm, lanes_ref, loc.at[14]),
        pltpu.make_async_copy(qkv_hbm, wt.at[pl.ds(0, 96)], loc.at[15]),
        pltpu.make_async_copy(selfo_hbm, wt.at[pl.ds(96, 32)], loc.at[16]),
    ]
    for copy in local:
        copy.start()

    for n in (10, 9, 8, 14):
        local[n].wait()

    lim_nat[...] = jnp.broadcast_to(limits_ref[...].astype(F32), (128, 256)).T
    for c_of in range(2):
        for x_of in range(2):
            for z_of in range(8):
                slot = ((c_of * 2 + x_of) * 8 + z_of) * 8
                row = (z_of * 4 + x_of * 2 + c_of) * 8
                lim_perm[slot : slot + 8, :] = lim_nat[row : row + 8, :]

    local[0].wait()
    raw = dot(states_ref[...], crossq[...])
    period, inverse, factor = lanes_ref[0:1, :], lanes_ref[1:2, :], lanes_ref[2:3, :]
    position = lim_nat[pl.ds(pl.multiple_of(8 * me, 8), 8), :] - 1.0
    phase = position - jnp.floor(position * inverse) * period
    phase = jnp.where(phase < 0.0, phase + period, phase)
    phase = jnp.where(phase >= period, phase - period, phase) * factor
    lane8 = iota((8, 128), 1)
    first = lax.rem(lane8, 64) < 32
    cosines = jnp.cos(phase)
    sines = jnp.sin(phase)
    sines = jnp.where(first, -sines, sines)
    for p in range(8):
        tile = raw[:, 128 * p : 128 * p + 128]
        swapped = jnp.where(first, pltpu.roll(tile, 96, 1), pltpu.roll(tile, 32, 1))
        qsrc[p] = (tile * cosines + swapped * sines).astype(BF16).astype(F32) * 0.125
    qbuf[core, x * 8 + z] = qsrc[z]
    ids_all[chip] = ids_ref[...]
    packed = states_ref[...].astype(F32)
    packed = jnp.concatenate([packed[:, :512], packed[:, 512:]], axis=0).astype(BF16)
    stpack[...] = packed
    strecv[z] = packed

    pl.semaphore_wait(barrier, 21)

    def send_ids(i):
        k = same_core(i)
        remote(ids_ref, ids_all.at[chip], ss.at[0], rs.at[0], 2 * k + core).start()
        remote(qsrc.at[k // 2], qbuf.at[core, x * 8 + z], ss.at[1], rs.at[1], 2 * k + core).start()

    over(16, send_ids)

    def ring(i):
        return lax.rem(me + 4 * i, 32)

    over(8, lambda i: remote(stpack, strecv.at[z], ss.at[2], rs.at[2], ring(i)).start())
    local[16].wait()

    def send_selfo(i):
        remote(wt.at[pl.ds(96, 32)], selfo.at[chip, core], ss.at[13], rs.at[3], ring(i)).start()

    @pl.when(carrier)
    def _():
        selfo[chip, core] = wt[96:128, :]
        over(8, send_selfo)

    own_up = [
        remote(up_hbm, updown_up.at[quad], ss.at[3], rs_up.at[quad], sib),
        remote(down_hbm, updown_dn.at[quad], ss.at[4], rs_dn.at[quad], sib),
        remote(up_hbm, updown_up.at[quad], ss.at[5], rs_up.at[quad], across, dp_pair),
        remote(down_hbm, updown_dn.at[quad], ss.at[6], rs_dn.at[quad], across, dp_pair),
    ]
    for copy in own_up:
        copy.start()

    local[1].wait()
    local[2].wait()
    local[3].wait()
    local[4].wait()
    local[13].wait()
    key_rows = dot(embed[...], ck[...]).T
    key_rows = jnp.where(x == 0, key_rows[0:64], key_rows[64:128])
    value_rows = dot(embed[...], cv[...]).T
    value_rows = jnp.where(x == 0, value_rows[0:64], value_rows[64:128])
    key_top = key_rows.astype(BF16)
    key_rest = (key_rows - key_top.astype(F32)).astype(BF16)
    table = jnp.concatenate([key_top, key_rest, value_rows.astype(BF16)], axis=0)

    def wait_in(buf, sem):
        pltpu.make_async_copy(buf, buf, sem).wait()

    wait_in(ids_all.at[pl.ds(0, 15)], rs.at[0])
    wait_in(qbuf.at[core, pl.ds(0, 15)], rs.at[1])
    forward_q = remote(qbuf.at[core], qbuf.at[core], ss.at[14], rs.at[4], sib)
    forward_q.start()
    wait_in(qbuf.at[1 - core], rs.at[4])

    local[15].wait()

    def unit_copies(i):
        unit = 3 * me + i
        index = 4 * (unit // 32) + lax.rem(unit, 4)
        target = 4 * (lax.rem(unit, 32) // 4) + quad
        away = remote(wt.at[pl.ds(32 * i, 32)], wqkv.at[index], ss.at[7 + i], rs_w.at[index], target)
        here = pltpu.make_async_copy(wt.at[pl.ds(32 * i, 32)], wqkv.at[index], rs_w.at[index])
        return target, away, here

    for i in range(3):
        target, away, here = unit_copies(i)
        pl.when(target != me)(away.start)
        pl.when(target == me)(here.start)

    lane256 = iota((256, 128), 1)
    queries = jnp.where(lane256 // 64 == x, qbuf[...].reshape(256, 128), 0.0).astype(BF16)
    acc[...] = jnp.zeros((256, 128), F32)
    peak[...] = jnp.full((256, 128), LOW, F32)

    def context_block(j, masked):
        block = 2 * j + core
        onehot = (iota((256, 1024), 0) == ids_all[j]).astype(F32).astype(BF16)
        rows = dot(table, onehot)
        keys = rows[0:64] + rows[64:128]
        here = jnp.where(iota((64, 128), 1) == block, start_ref[...], 0.0)
        here = jnp.sum(here, axis=1, keepdims=True)
        cos_a, sin_a, cos_b, sin_b = here[0:32], here[32:64], base[0:32, :], base[32:64, :]
        cos = cos_a * cos_b - sin_a * sin_b
        sin = sin_a * cos_b + cos_a * sin_b
        one, two = keys[0:32], keys[32:64]
        turned = jnp.concatenate([one * cos - two * sin, two * cos + one * sin], axis=0)
        turned = turned.astype(BF16)
        scores = dot(queries, jnp.concatenate([turned, turned], axis=0))
        if masked:
            place = (block * 1024 + iota((1, 1024), 1)).astype(F32)
            scores = jnp.where(place < lim_perm[:, 0:1], scores, LOW)
        top = jnp.max(scores, axis=1, keepdims=True)
        weights = jnp.exp(scores - top).astype(BF16)
        values = jnp.concatenate([rows[128:192].astype(BF16), jnp.ones((64, 1024), BF16)], axis=0)
        terms = dot_nt(weights, values)
        old = peak[...]
        new = jnp.maximum(old, top)
        acc[...] = acc[...] * jnp.exp(old - new) + terms * jnp.exp(top - new)
        peak[...] = new

    lax.fori_loop(0, 8, lambda j, carry: (context_block(j, False), carry)[1], 0, unroll=4)

    lax.fori_loop(8, 12, lambda j, carry: (context_block(j, True), carry)[1], 0, unroll=4)

    @pl.when(carrier)
    def _():
        wait_in(selfo.at[pl.ds(0, 1), 0], rs.at[3])

    @pl.when(jnp.logical_not(carrier))
    def _():
        wait_in(selfo.at[pl.ds(0, 2), 0], rs.at[3])

    along_x = []
    for n in range(2):
        brought = selfo.at[2 * y + 8 * n + x, core]
        along_x.append(remote(brought, brought, ss.at[43 + n], rs.at[11], across, dp_pair))
    for copy in along_x:
        copy.start()

    def unit_quad(index):
        unit = 32 * (index // 4) + 4 * z + index % 4
        return lax.rem(unit // 3, 4)

    def unit_across(index):
        return remote(wqkv.at[index], wqkv.at[index], ss.at[45 + index], rs_w.at[index], across, dp_pair)

    def unit_forward(index):
        return remote(wqkv.at[index], wqkv.at[index], ss.at[18 + index], rs_w.at[index], sib)

    def turn_unit(index):
        wait_in(wqkv.at[index], rs_w.at[index])
        unit_across(index).start()
        unit_forward(index).start()

    for index in range(12):
        pl.when(unit_quad(index) == quad)(lambda index=index: turn_unit(index))

    lax.fori_loop(12, 16, lambda j, carry: (context_block(j, True), carry)[1], 0, unroll=4)

    wait_in(selfo.at[pl.ds(0, 2), 0], rs.at[11])
    along_y = []
    for i in range(1, 4):
        for n in range(2):
            brought = selfo.at[pl.ds(2 * y + 8 * n, 2), core]
            sem = ss.at[37 + 2 * (i - 1) + n]
            along_y.append(remote(brought, brought, sem, rs.at[10], me, lax.rem(dp + 2 * i, 8)))
    for copy in along_y:
        copy.start()


    packs[...] = jnp.where(lane256 == 127, peak[...], acc[...]).reshape(2, 128, 128)
    swap = remote(packs.at[1 - core], comb, ss.at[15], rs.at[5], sib)
    swap.start()

    wait_in(updown_up.at[quad_x], rs_up.at[quad_x])
    wait_in(updown_dn.at[quad_x], rs_dn.at[quad_x])
    forwards = [
        remote(updown_up.at[quad_x], updown_up.at[quad_x], ss.at[16], rs_up.at[quad_x], sib),
        remote(updown_dn.at[quad_x], updown_dn.at[quad_x], ss.at[17], rs_dn.at[quad_x], sib),
    ]
    for copy in forwards:
        copy.start()

    def pass_unit(index):
        wait_in(wqkv.at[index], rs_w.at[index])
        unit_forward(index).start()

    for index in range(12):
        pl.when(unit_quad(index) == quad_x)(lambda index=index: pass_unit(index))

    wait_in(comb, rs.at[5])
    mine, theirs = packs[core], comb[...]
    peak_a, peak_b = mine[:, 127:128], theirs[:, 127:128]
    top = jnp.maximum(peak_a, peak_b)
    both = mine * jnp.exp(peak_a - top) + theirs * jnp.exp(peak_b - top)
    mixed = both / both[:, 64:65]
    lane32 = iota((32, 128), 1)
    for x_of in range(2):
        low, high = mixed[64 * x_of : 64 * x_of + 32], mixed[64 * x_of + 32 : 64 * x_of + 64]
        mixsrc[x_of] = jnp.where(lane32 < 64, low, pltpu.roll(high, 64, 1)).astype(BF16)
    mixrecv[chip] = mixsrc[x]

    def send_mix(i):
        k = same_core(i)
        remote(mixsrc.at[lax.rem(k, 2)], mixrecv.at[chip], ss.at[30], rs.at[6], 2 * k + core).start()

    over(16, send_mix)

    wait_in(strecv.at[pl.ds(0, 7)], rs.at[2])
    for z_of in range(8):
        rows = strecv[z_of].astype(F32)
        lat[8 * z_of : 8 * z_of + 8, :] = jnp.concatenate([rows[0:8], rows[8:16]], axis=1)
    for index in range(12):
        pl.when(lax.rem(unit_quad(index), 2) != core)(
            lambda index=index: wait_in(wqkv.at[index], rs_w.at[index])
        )
    local[7].wait()
    local[11].wait()
    local[12].wait()
    wait_in(mixrecv.at[pl.ds(0, 15)], rs.at[6])
    for p in range(8):
        even, odd = mixrecv[2 * p].astype(F32), mixrecv[2 * p + 1].astype(F32)
        above = jnp.where(lane32 < 64, even, pltpu.roll(odd, 64, 1))
        below = jnp.where(lane32 < 64, pltpu.roll(even, 64, 1), odd)
        mixf[:, 128 * p : 128 * p + 128] = jnp.concatenate([above, below], axis=0).astype(BF16)
    latents = lat[...] + dot(mixf[...], crosso[...])
    normed = rms_scale(latents, attn_gain[...]).astype(BF16)
    lat[...] = latents

    projected = dot_nt(normed, wqkv[...].reshape(384, 1024)).astype(BF16)
    kvall[quad] = projected[:, 128:384]
    kv_copies = [
        remote(kvall.at[quad], kvall.at[quad], ss.at[32 + n], rs_kv.at[quad], seq)
        for n, seq in enumerate((sib, across, diagonal))
    ]
    for copy in kv_copies:
        copy.start()
    wait_in(selfo.at[pl.ds(0, 12), 0], rs.at[10])
    forward_o = remote(selfo.at[:, core], selfo.at[:, core], ss.at[31], rs.at[7], sib)
    forward_o.start()

    for other in (1, 2, 3):
        slot = lax.rem(quad + other, 4)
        wait_in(kvall.at[slot], rs_kv.at[slot])
    lane64 = iota((64, 128), 1)
    keys = kvall[:, :, 0:128].reshape(256, 128)
    values = kvall[:, :, 128:256].reshape(256, 128)
    key_lane = iota((64, 256), 1)
    key_row = 32 * (lax.rem(key_lane, 64) // 8) + 8 * (key_lane // 64) + lax.rem(key_lane, 8)
    query_at = iota((64, 256), 0)
    query_row = 32 * (query_at // 8) + 8 * quad + lax.rem(query_at, 8)
    causal = key_row <= query_row
    heads = []
    for head in range(2):
        only = jnp.where(lane64 // 64 == head, projected[:, 0:128].astype(F32), 0.0).astype(BF16)
        scores = jnp.where(causal, dot_nt(only, keys) * 0.125, LOW)
        weights = jnp.exp(scores - jnp.max(scores, axis=1, keepdims=True))
        total = jnp.sum(weights, axis=1, keepdims=True)
        coarse = weights.astype(BF16)
        fine = (weights - coarse.astype(F32)).astype(BF16)
        heads.append((dot(coarse, values) + dot(fine, values)) / total)
    mix2all[z] = jnp.where(lane64 < 64, heads[0], heads[1]).astype(BF16)
    over(8, lambda i: remote(mix2all.at[z], mix2all.at[z], ss.at[35], rs.at[8], ring(i)).start())
    wait_in(selfo.at[:, 1 - core], rs.at[7])
    wait_in(mix2all.at[pl.ds(0, 7)], rs.at[8])
    mix2 = jnp.concatenate([mix2all[k] for k in range(8)], axis=1)
    attended = lat[...] + dot_nt(mix2, selfo[...].reshape(1024, 1024))
    atts[...] = attended.reshape(8, 8, 1024)
    normed = rms_scale(attended, mlp_gain[...]).astype(BF16)

    local[5].wait()
    local[6].wait()
    for slot in (quad + 1 - 2 * core, quad_x + 1 - 2 * core):
        wait_in(updown_up.at[slot], rs_up.at[slot])
        wait_in(updown_dn.at[slot], rs_dn.at[slot])
    hidden = []
    for half in range(2):
        ups = jnp.concatenate([updown_up[2 * half], updown_up[2 * half + 1]], axis=1)
        hidden.append(jax.nn.gelu(dot(normed, ups), approximate=True).astype(BF16))
    hidden = jnp.concatenate(hidden, axis=1)
    part[...] = dot(hidden, updown_dn[...].reshape(512, 1024)).reshape(8, 8, 1024)
    precv[z] = part[z]

    def send_part(i):
        seq = ring(i)
        remote(part.at[seq // 4], precv.at[z], ss.at[36], rs.at[9], seq).start()

    over(8, send_part)
    wait_in(precv.at[pl.ds(0, 7)], rs.at[9])
    total = atts[z]
    summed = precv[0]
    for k in range(1, 8):
        summed = summed + precv[k]
    out_ref[...] = total + summed

    def wait_out(buf, sem):
        pltpu.make_async_copy(buf, buf, sem).wait()

    wait_out(ids_all.at[pl.ds(0, 15)], ss.at[0])
    wait_out(qbuf.at[0, pl.ds(0, 15)], ss.at[1])
    wait_out(strecv.at[pl.ds(0, 7)], ss.at[2])
    for copy in own_up + forwards + kv_copies + along_x + along_y + [forward_q, swap, forward_o]:
        copy.wait_send()
    for i in range(3):
        target, away, _ = unit_copies(i)
        pl.when(target != me)(away.wait_send)
    for index in range(12):
        pl.when(lax.rem(unit_quad(index), 2) == core)(
            lambda index=index: unit_forward(index).wait_send()
        )
        pl.when(unit_quad(index) == quad)(lambda index=index: unit_across(index).wait_send())

    @pl.when(carrier)
    def _():
        wait_out(selfo.at[pl.ds(0, 7), 0], ss.at[13])

    wait_out(mixrecv.at[pl.ds(0, 15)], ss.at[30])
    wait_out(mix2all.at[pl.ds(0, 7)], ss.at[35])
    wait_out(precv.at[pl.ds(0, 7)], ss.at[36])


def on_device(
    context_ids, embed_table, latent_states, limits, cross_q, cross_kv, cross_o,
    attn_gain, self_qkv, self_o, mlp_gain, mlp_up, mlp_down,
):
    base, start, lanes = trig_tables()
    vmem = pl.BlockSpec(memory_space=pltpu.VMEM)
    dma = pltpu.SemaphoreType.DMA
    return pl.pallas_call(
        kernel,
        out_shape=jax.ShapeDtypeStruct((8, 1024), F32),
        in_specs=[pl.BlockSpec(memory_space=pltpu.HBM)] * 16,
        out_specs=vmem,
        scratch_shapes=[
            pltpu.VMEM((1, 1024), jnp.int32),
            pltpu.VMEM((8, 1024), BF16),
            pltpu.VMEM((1, 256), jnp.int32),
            pltpu.VMEM((1, 1024), F32),
            pltpu.VMEM((1, 1024), F32),
            pltpu.VMEM((64, 128), F32),
            pltpu.VMEM((8, 128), F32),
            pltpu.VMEM((1024, 1024), BF16),
            pltpu.VMEM((256, 1024), BF16),
            pltpu.VMEM((1024, 128), BF16),
            pltpu.VMEM((1024, 128), BF16),
            pltpu.VMEM((64, 1024), F32),
            pltpu.VMEM((1024, 1024), BF16),
            pltpu.VMEM((4, 1024, 128), BF16),
            pltpu.VMEM((4, 128, 1024), BF16),
            pltpu.VMEM((256, 128), F32),
            pltpu.VMEM((256, 128), F32),
            pltpu.VMEM((8, 8, 128), F32),
            pltpu.VMEM((2, 16, 8, 128), F32),
            pltpu.VMEM((16, 1, 1024), jnp.int32),
            pltpu.VMEM((16, 512), BF16),
            pltpu.VMEM((8, 16, 512), BF16),
            pltpu.VMEM((128, 1024), BF16),
            pltpu.VMEM((12, 32, 1024), BF16),
            pltpu.VMEM((16, 2, 32, 1024), BF16),
            pltpu.VMEM((256, 128), F32),
            pltpu.VMEM((256, 128), F32),
            pltpu.VMEM((2, 128, 128), F32),
            pltpu.VMEM((128, 128), F32),
            pltpu.VMEM((2, 32, 128), BF16),
            pltpu.VMEM((16, 32, 128), BF16),
            pltpu.VMEM((64, 1024), BF16),
            pltpu.VMEM((64, 1024), F32),
            pltpu.VMEM((4, 64, 256), BF16),
            pltpu.VMEM((8, 64, 128), BF16),
            pltpu.VMEM((8, 8, 1024), F32),
            pltpu.VMEM((8, 8, 1024), F32),
            pltpu.VMEM((8, 8, 1024), F32),
            dma((17,)),
            dma((57,)),
            dma((12,)),
            dma((4,)),
            dma((4,)),
            dma((12,)),
            dma((4,)),
        ],
        compiler_params=pltpu.CompilerParams(
            collective_id=0, has_side_effects=True, vmem_limit_bytes=60 << 20
        ),
        name="ar_step",
    )(
        context_ids.reshape(1, -1), latent_states, limits.reshape(1, -1),
        attn_gain.reshape(1, -1), mlp_gain.reshape(1, -1), self_qkv.T, self_o.T,
        jnp.asarray(start), jnp.asarray(lanes), jnp.asarray(base),
        embed_table, cross_q, cross_kv, cross_o, mlp_up, mlp_down,
    )


def solution(mesh):
    placed = (
        P(("dp", "seq")),
        P(),
        P(("dp", "seq"), None),
        P("dp"),
        P(),
        P(),
        P(),
        P(),
        P(None, "seq"),
        P(None, "seq"),
        P(),
        P(None, "seq"),
        P("seq", None),
    )
    return jax.shard_map(
        on_device, mesh=mesh, in_specs=placed, out_specs=P(("dp", "seq"), None), check_vma=False
    )
```

```python
import math

import jax
import jax.numpy as jnp
import numpy as np
from jax import lax
from jax.experimental import pallas as pl
from jax.experimental.pallas import tpu as pltpu
from jax.sharding import PartitionSpec as P

F32 = jnp.float32
BF16 = jnp.bfloat16
MESH = pl.DeviceIdType.MESH
LOW = -1e30


def trig_tables():
    periods = np.array([int(4.0 * 16384.0 ** (f / 31)) for f in range(32)], np.int64)

    def angles(positions):
        return 2.0 * np.pi * (positions[None, :] % periods[:, None]) / periods[:, None]

    base = angles(np.arange(1024))
    base = np.concatenate([np.cos(base), np.sin(base)]).astype(np.float32)
    start = angles(np.arange(32) * 1024)
    start = np.concatenate([np.cos(start), np.sin(start)]).astype(np.float32)
    start = np.pad(start, ((0, 0), (0, 96)))
    by_lane = np.tile(periods, 4).astype(np.float64)
    lanes = np.zeros((8, 128), np.float32)
    lanes[0], lanes[1], lanes[2] = by_lane, 1.0 / by_lane, 2.0 * np.pi / by_lane
    return base, start, lanes


def dot(left, right):
    return lax.dot_general(left, right, (((1,), (0,)), ((), ())), preferred_element_type=F32)


def dot_nt(left, right):
    return lax.dot_general(left, right, (((1,), (1,)), ((), ())), preferred_element_type=F32)


def iota(shape, axis):
    return lax.broadcasted_iota(jnp.int32, shape, axis)


def rms_scale(states, gain):
    mean_sq = jnp.mean(states * states, axis=-1, keepdims=True)
    return states * lax.rsqrt(mean_sq + 1e-05) * gain


def kernel(
    ids_hbm, states_hbm, limits_hbm, attn_gain_hbm, mlp_gain_hbm, qkv_hbm, selfo_hbm, start_hbm, lanes_hbm,
    base_hbm, embed_hbm, crossq_hbm, crosskv_hbm, crosso_hbm, up_hbm, down_hbm,
    out_ref,
    ids_ref, states_ref, limits_ref, attn_gain, mlp_gain, start_ref, lanes_ref,
    crossq, embed, ck, cv, base, crosso, updown_up, updown_dn,
    lim_nat, lim_perm, qsrc, qbuf, ids_all, stpack, strecv, wt, wqkv, selfo,
    keys_at, values_at, acc, peak, packs, comb, mixsrc, mixrecv, mixf, lat, kvall, mix2all, atts, part, precv, whole,
    loc, ss, rs, rs_up, rs_dn, rs_w, rs_kv,
):
    me = lax.axis_index("seq")
    dp = lax.axis_index("dp")
    core = lax.rem(me, 2)
    chip = me // 2
    x = lax.rem(chip, 2)
    z = chip // 2
    quad = lax.rem(me, 4)
    sib = me + 1 - 2 * core
    across = me + 2 - 4 * x
    diagonal = sib + 2 - 4 * x
    dp_pair = dp + 1 - 2 * lax.rem(dp, 2)
    y = dp // 2
    carrier = lax.rem(z, 4) == y
    quad_x = quad + 2 - 4 * x

    offsets = [(dz, dx) for dz in (4, 3, 5, 2, 6, 1, 7, 0) for dx in (1, 0) if dz or dx]
    same_core = [2 * lax.rem(z + dz, 8) + lax.rem(x + dx, 2) for dz, dx in offsets]
    ring = [lax.rem(me + 4 * dz, 32) for dz in (4, 3, 5, 2, 6, 1, 7)]

    def remote(src, dst, send, recv, seq, part_of=None):
        where = {"seq": seq} if part_of is None else {"dp": part_of, "seq": seq}
        return pltpu.make_async_remote_copy(
            src_ref=src, dst_ref=dst, send_sem=send, recv_sem=recv, device_id=where, device_id_type=MESH
        )

    def over(targets, body):
        for target in targets:
            body(target)

    barrier = pltpu.get_barrier_semaphore()

    def greet(seq, part_of=None):
        where = {"seq": seq} if part_of is None else {"dp": part_of, "seq": seq}
        pl.semaphore_signal(barrier, inc=1, device_id=where, device_id_type=MESH)

    over(same_core, lambda k: greet(2 * k + core))
    greet(sib)
    greet(diagonal)
    greet(across, dp_pair)
    over((1, 2, 3), lambda i: greet(me, lax.rem(dp + 2 * i, 8)))

    columns = pl.multiple_of(128 * z, 128)
    local = [
        pltpu.make_async_copy(crossq_hbm, crossq, loc.at[0]),
        pltpu.make_async_copy(embed_hbm, embed, loc.at[1]),
        pltpu.make_async_copy(crosskv_hbm.at[:, pl.ds(columns, 128)], ck, loc.at[2]),
        pltpu.make_async_copy(crosskv_hbm.at[:, pl.ds(columns + 1024, 128)], cv, loc.at[3]),
        pltpu.make_async_copy(base_hbm, base, loc.at[4]),
        pltpu.make_async_copy(up_hbm, updown_up.at[quad], loc.at[5]),
        pltpu.make_async_copy(down_hbm, updown_dn.at[quad], loc.at[6]),
        pltpu.make_async_copy(crosso_hbm, crosso, loc.at[7]),
        pltpu.make_async_copy(ids_hbm, ids_ref, loc.at[8]),
        pltpu.make_async_copy(states_hbm, states_ref, loc.at[9]),
        pltpu.make_async_copy(limits_hbm, limits_ref, loc.at[10]),
        pltpu.make_async_copy(attn_gain_hbm, attn_gain, loc.at[11]),
        pltpu.make_async_copy(mlp_gain_hbm, mlp_gain, loc.at[12]),
        pltpu.make_async_copy(start_hbm, start_ref, loc.at[13]),
        pltpu.make_async_copy(lanes_hbm, lanes_ref, loc.at[14]),
        pltpu.make_async_copy(qkv_hbm, wt.at[pl.ds(0, 96)], loc.at[15]),
        pltpu.make_async_copy(selfo_hbm, wt.at[pl.ds(96, 32)], loc.at[16]),
    ]
    for copy in local:
        copy.start()

    for n in (10, 9, 8, 14):
        local[n].wait()

    lim_nat[...] = jnp.broadcast_to(limits_ref[...].astype(F32), (128, 256)).T
    for c_of in range(2):
        for x_of in range(2):
            for z_of in range(8):
                slot = ((c_of * 2 + x_of) * 8 + z_of) * 8
                row = (z_of * 4 + x_of * 2 + c_of) * 8
                lim_perm[slot : slot + 8, :] = lim_nat[row : row + 8, :]

    local[0].wait()
    raw = dot(states_ref[...], crossq[...])
    period, inverse, factor = lanes_ref[0:1, :], lanes_ref[1:2, :], lanes_ref[2:3, :]
    position = lim_nat[pl.ds(pl.multiple_of(8 * me, 8), 8), :] - 1.0
    phase = position - jnp.floor(position * inverse) * period
    phase = jnp.where(phase < 0.0, phase + period, phase)
    phase = jnp.where(phase >= period, phase - period, phase) * factor
    lane8 = iota((8, 128), 1)
    first = lax.rem(lane8, 64) < 32
    cosines = jnp.cos(phase)
    sines = jnp.sin(phase)
    sines = jnp.where(first, -sines, sines)
    for p in range(8):
        tile = raw[:, 128 * p : 128 * p + 128]
        swapped = jnp.where(first, pltpu.roll(tile, 96, 1), pltpu.roll(tile, 32, 1))
        qsrc[p] = (tile * cosines + swapped * sines).astype(BF16).astype(F32) * 0.125
    qbuf[core, x * 8 + z] = qsrc[z]
    ids_all[chip] = ids_ref[...]
    packed = states_ref[...].astype(F32)
    packed = jnp.concatenate([packed[:, :512], packed[:, 512:]], axis=0).astype(BF16)
    stpack[...] = packed
    strecv[z] = packed

    pl.semaphore_wait(barrier, 21)

    def send_ids(k):
        remote(ids_ref, ids_all.at[chip], ss.at[0], rs.at[0], 2 * k + core).start()

    def send_queries(k):
        remote(qsrc.at[k // 2], qbuf.at[core, x * 8 + z], ss.at[1], rs.at[1], 2 * k + core).start()

    over(same_core, send_ids)
    over(same_core, send_queries)

    over(ring, lambda seq: remote(stpack, strecv.at[z], ss.at[2], rs.at[2], seq).start())
    local[16].wait()

    def send_selfo(seq):
        remote(wt.at[pl.ds(96, 32)], selfo.at[chip, core], ss.at[13], rs.at[3], seq).start()

    @pl.when(carrier)
    def _():
        selfo[chip, core] = wt[96:128, :]
        over(ring, send_selfo)

    local[15].wait()

    def unit_copies(i):
        unit = 3 * me + i
        index = 4 * (unit // 32) + lax.rem(unit, 4)
        target = 4 * (lax.rem(unit, 32) // 4) + quad
        away = remote(wt.at[pl.ds(32 * i, 32)], wqkv.at[index], ss.at[7 + i], rs_w.at[index], target)
        here = pltpu.make_async_copy(wt.at[pl.ds(32 * i, 32)], wqkv.at[index], rs_w.at[index])
        return target, away, here

    for i in range(3):
        target, away, here = unit_copies(i)
        pl.when(target != me)(away.start)
        pl.when(target == me)(here.start)

    own_up = [
        remote(up_hbm, updown_up.at[quad], ss.at[3], rs_up.at[quad], sib),
        remote(down_hbm, updown_dn.at[quad], ss.at[4], rs_dn.at[quad], sib),
        remote(up_hbm, updown_up.at[quad], ss.at[5], rs_up.at[quad], across, dp_pair),
        remote(down_hbm, updown_dn.at[quad], ss.at[6], rs_dn.at[quad], across, dp_pair),
    ]
    for copy in own_up:
        copy.start()

    local[1].wait()
    local[2].wait()
    local[3].wait()
    local[4].wait()
    local[13].wait()
    key_rows = dot(embed[...], ck[...]).T
    key_rows = jnp.where(x == 0, key_rows[0:64], key_rows[64:128])
    value_rows = dot(embed[...], cv[...]).T
    value_rows = jnp.where(x == 0, value_rows[0:64], value_rows[64:128])
    key_top = key_rows.astype(BF16)
    key_rest = (key_rows - key_top.astype(F32)).astype(BF16)
    table = jnp.concatenate([key_top, key_rest, value_rows.astype(BF16)], axis=0)

    def wait_in(buf, sem):
        pltpu.make_async_copy(buf, buf, sem).wait()

    wait_in(ids_all.at[pl.ds(0, 15)], rs.at[0])
    def key_block(j, slot):
        block = 2 * j + core
        ids = jnp.broadcast_to(ids_all[j].astype(F32).astype(BF16), (256, 1024))
        onehot = jnp.where(iota((256, 1024), 0).astype(F32).astype(BF16) == ids, 1.0, 0.0).astype(BF16)
        rows = dot(table, onehot)
        keys = rows[0:64] + rows[64:128]
        here = jnp.where(iota((64, 128), 1) == block, start_ref[...], 0.0)
        here = jnp.sum(here, axis=1, keepdims=True)
        cos_a, sin_a, cos_b, sin_b = here[0:32], here[32:64], base[0:32, :], base[32:64, :]
        cos = cos_a * cos_b - sin_a * sin_b
        sin = sin_a * cos_b + cos_a * sin_b
        one, two = keys[0:32], keys[32:64]
        turned = jnp.concatenate([one * cos - two * sin, two * cos + one * sin], axis=0)
        keys_at[slot] = turned.astype(BF16)
        values_at[slot] = rows[128:192].astype(BF16)

    for slot in range(4):
        key_block(slot, slot)
    wait_in(qbuf.at[core, pl.ds(0, 15)], rs.at[1])
    forward_q = remote(qbuf.at[core], qbuf.at[core], ss.at[14], rs.at[4], sib)
    forward_q.start()
    wait_in(qbuf.at[1 - core], rs.at[4])
    lane256 = iota((256, 128), 1)
    queries = jnp.where(lane256 // 64 == x, qbuf[...].reshape(256, 128), 0.0).astype(BF16)
    acc[...] = jnp.zeros((256, 128), F32)
    peak[...] = jnp.full((256, 128), LOW, F32)

    def context_block(j, slot, masked):
        block = 2 * j + core
        turned = keys_at[slot]
        scores = dot(queries, jnp.concatenate([turned, turned], axis=0))
        if masked:
            place = (block * 1024 + iota((1, 1024), 1)).astype(F32)
            scores = jnp.where(place < lim_perm[:, 0:1], scores, LOW)
        top = jnp.max(scores, axis=1, keepdims=True)
        weights = jnp.exp(scores - top).astype(BF16)
        values = jnp.concatenate([values_at[slot], jnp.ones((64, 1024), BF16)], axis=0)
        terms = dot_nt(weights, values)
        old = peak[...]
        new = jnp.maximum(old, top)
        acc[...] = acc[...] * jnp.exp(old - new) + terms * jnp.exp(top - new)
        peak[...] = new

    @pl.loop(0, 8, step=4)
    def _(start):
        for slot in range(4):
            context_block(start + slot, slot, False)
            key_block(start + slot + 4, slot)

    @pl.loop(8, 12, step=4)
    def _(start):
        for slot in range(4):
            context_block(start + slot, slot, True)
            key_block(start + slot + 4, slot)

    @pl.when(carrier)
    def _():
        wait_in(selfo.at[pl.ds(0, 1), 0], rs.at[3])

    @pl.when(jnp.logical_not(carrier))
    def _():
        wait_in(selfo.at[pl.ds(0, 2), 0], rs.at[3])

    along_x = []
    for n in range(2):
        brought = selfo.at[2 * y + 8 * n + x, core]
        along_x.append(remote(brought, brought, ss.at[43 + n], rs.at[11], across, dp_pair))
    for copy in along_x:
        copy.start()

    def unit_quad(index):
        unit = 32 * (index // 4) + 4 * z + index % 4
        return lax.rem(unit // 3, 4)

    def unit_across(index):
        return remote(wqkv.at[index], wqkv.at[index], ss.at[45 + index], rs_w.at[index], across, dp_pair)

    def unit_forward(index):
        return remote(wqkv.at[index], wqkv.at[index], ss.at[18 + index], rs_w.at[index], sib)

    def turn_unit(index):
        wait_in(wqkv.at[index], rs_w.at[index])
        unit_across(index).start()
        unit_forward(index).start()

    for index in range(12):
        pl.when(unit_quad(index) == quad)(lambda index=index: turn_unit(index))

    @pl.loop(12, 16, step=4)
    def _(start):
        for slot in range(4):
            context_block(start + slot, slot, True)

    wait_in(selfo.at[pl.ds(0, 2), 0], rs.at[11])
    along_y = []
    for i in range(1, 4):
        for n in range(2):
            brought = selfo.at[pl.ds(2 * y + 8 * n, 2), core]
            sem = ss.at[37 + 2 * (i - 1) + n]
            along_y.append(remote(brought, brought, sem, rs.at[10], me, lax.rem(dp + 2 * i, 8)))
    for copy in along_y:
        copy.start()


    packs[...] = jnp.where(lane256 == 127, peak[...], acc[...]).reshape(2, 128, 128)
    swap = remote(packs.at[1 - core], comb, ss.at[15], rs.at[5], sib)
    swap.start()

    wait_in(updown_up.at[quad_x], rs_up.at[quad_x])
    wait_in(updown_dn.at[quad_x], rs_dn.at[quad_x])
    forwards = [
        remote(updown_up.at[quad_x], updown_up.at[quad_x], ss.at[16], rs_up.at[quad_x], sib),
        remote(updown_dn.at[quad_x], updown_dn.at[quad_x], ss.at[17], rs_dn.at[quad_x], sib),
    ]
    for copy in forwards:
        copy.start()

    def pass_unit(index):
        wait_in(wqkv.at[index], rs_w.at[index])
        unit_forward(index).start()

    for index in range(12):
        pl.when(unit_quad(index) == quad_x)(lambda index=index: pass_unit(index))

    wait_in(comb, rs.at[5])
    mine, theirs = packs[core], comb[...]
    peak_a, peak_b = mine[:, 127:128], theirs[:, 127:128]
    top = jnp.maximum(peak_a, peak_b)
    both = mine * jnp.exp(peak_a - top) + theirs * jnp.exp(peak_b - top)
    mixed = both / both[:, 64:65]
    lane32 = iota((32, 128), 1)
    for x_of in range(2):
        low, high = mixed[64 * x_of : 64 * x_of + 32], mixed[64 * x_of + 32 : 64 * x_of + 64]
        mixsrc[x_of] = jnp.where(lane32 < 64, low, pltpu.roll(high, 64, 1)).astype(BF16)
    mixrecv[chip] = mixsrc[x]

    def send_mix(k):
        remote(mixsrc.at[lax.rem(k, 2)], mixrecv.at[chip], ss.at[30], rs.at[6], 2 * k + core).start()

    over(same_core, send_mix)

    wait_in(strecv.at[pl.ds(0, 7)], rs.at[2])
    for z_of in range(8):
        rows = strecv[z_of].astype(F32)
        lat[8 * z_of : 8 * z_of + 8, :] = jnp.concatenate([rows[0:8], rows[8:16]], axis=1)
    for index in range(12):
        pl.when(lax.rem(unit_quad(index), 2) != core)(
            lambda index=index: wait_in(wqkv.at[index], rs_w.at[index])
        )
    local[7].wait()
    local[11].wait()
    local[12].wait()
    wait_in(mixrecv.at[pl.ds(0, 15)], rs.at[6])
    for p in range(8):
        even, odd = mixrecv[2 * p].astype(F32), mixrecv[2 * p + 1].astype(F32)
        above = jnp.where(lane32 < 64, even, pltpu.roll(odd, 64, 1))
        below = jnp.where(lane32 < 64, pltpu.roll(even, 64, 1), odd)
        mixf[:, 128 * p : 128 * p + 128] = jnp.concatenate([above, below], axis=0).astype(BF16)
    latents = lat[...] + dot(mixf[...], crosso[...])
    normed = rms_scale(latents, attn_gain[...]).astype(BF16)
    lat[...] = latents

    projected = dot_nt(normed, wqkv[...].reshape(384, 1024)).astype(BF16)
    kvall[quad] = projected[:, 128:384]
    kv_copies = [
        remote(kvall.at[quad], kvall.at[quad], ss.at[32 + n], rs_kv.at[quad], seq)
        for n, seq in enumerate((sib, across, diagonal))
    ]
    for copy in kv_copies:
        copy.start()
    wait_in(selfo.at[pl.ds(0, 12), 0], rs.at[10])
    forward_o = remote(selfo.at[:, core], selfo.at[:, core], ss.at[31], rs.at[7], sib)
    forward_o.start()

    for other in (1, 2, 3):
        slot = lax.rem(quad + other, 4)
        wait_in(kvall.at[slot], rs_kv.at[slot])
    lane64 = iota((64, 128), 1)
    keys = kvall[:, :, 0:128].reshape(256, 128)
    values = kvall[:, :, 128:256].reshape(256, 128)
    key_lane = iota((64, 256), 1)
    key_row = 32 * (lax.rem(key_lane, 64) // 8) + 8 * (key_lane // 64) + lax.rem(key_lane, 8)
    query_at = iota((64, 256), 0)
    query_row = 32 * (query_at // 8) + 8 * quad + lax.rem(query_at, 8)
    causal = key_row <= query_row
    heads = []
    for head in range(2):
        only = jnp.where(lane64 // 64 == head, projected[:, 0:128].astype(F32), 0.0).astype(BF16)
        scores = jnp.where(causal, dot_nt(only, keys) * 0.125, LOW)
        weights = jnp.exp(scores - jnp.max(scores, axis=1, keepdims=True))
        total = jnp.sum(weights, axis=1, keepdims=True)
        coarse = weights.astype(BF16)
        fine = (weights - coarse.astype(F32)).astype(BF16)
        heads.append((dot(coarse, values) + dot(fine, values)) / total)
    mix2all[z] = jnp.where(lane64 < 64, heads[0], heads[1]).astype(BF16)
    over(ring, lambda seq: remote(mix2all.at[z], mix2all.at[z], ss.at[35], rs.at[8], seq).start())
    wait_in(selfo.at[:, 1 - core], rs.at[7])
    wait_in(mix2all.at[pl.ds(0, 7)], rs.at[8])
    mix2 = jnp.concatenate([mix2all[k] for k in range(8)], axis=1)
    attended = lat[...] + dot_nt(mix2, selfo[...].reshape(1024, 1024))
    atts[...] = attended.reshape(8, 8, 1024)
    normed = rms_scale(attended, mlp_gain[...]).astype(BF16)

    local[5].wait()
    local[6].wait()
    for slot in (quad + 1 - 2 * core, quad_x + 1 - 2 * core):
        wait_in(updown_up.at[slot], rs_up.at[slot])
        wait_in(updown_dn.at[slot], rs_dn.at[slot])
    hidden = []
    for half in range(2):
        ups = jnp.concatenate([updown_up[2 * half], updown_up[2 * half + 1]], axis=1)
        hidden.append(jax.nn.gelu(dot(normed, ups), approximate=True).astype(BF16))
    hidden = jnp.concatenate(hidden, axis=1)
    terms = dot(hidden, updown_dn[...].reshape(512, 1024))
    for k in range(8):
        rows = terms[8 * k : 8 * k + 8]
        part[k] = jnp.concatenate([rows[:, :512], rows[:, 512:]], axis=0).astype(BF16)

    def send_part(seq):
        remote(part.at[seq // 4], precv.at[z], ss.at[36], rs.at[9], seq).start()

    over(ring, send_part)
    whole[...] = terms.reshape(8, 8, 1024)
    own = whole[z]
    precv[z] = jnp.zeros((16, 512), BF16)
    wait_in(precv.at[pl.ds(0, 7)], rs.at[9])
    summed = precv[0].astype(F32)
    for k in range(1, 8):
        summed = summed + precv[k].astype(F32)
    out_ref[...] = atts[z] + (own + jnp.concatenate([summed[:8], summed[8:]], axis=1))

    def wait_out(buf, sem):
        pltpu.make_async_copy(buf, buf, sem).wait()

    wait_out(ids_all.at[pl.ds(0, 15)], ss.at[0])
    wait_out(qbuf.at[0, pl.ds(0, 15)], ss.at[1])
    wait_out(strecv.at[pl.ds(0, 7)], ss.at[2])
    for copy in own_up + forwards + kv_copies + along_x + along_y + [forward_q, swap, forward_o]:
        copy.wait_send()
    for i in range(3):
        target, away, _ = unit_copies(i)
        pl.when(target != me)(away.wait_send)
    for index in range(12):
        pl.when(lax.rem(unit_quad(index), 2) == core)(
            lambda index=index: unit_forward(index).wait_send()
        )
        pl.when(unit_quad(index) == quad)(lambda index=index: unit_across(index).wait_send())

    @pl.when(carrier)
    def _():
        wait_out(selfo.at[pl.ds(0, 7), 0], ss.at[13])

    wait_out(mixrecv.at[pl.ds(0, 15)], ss.at[30])
    wait_out(mix2all.at[pl.ds(0, 7)], ss.at[35])
    wait_out(precv.at[pl.ds(0, 7)], ss.at[36])


def on_device(
    context_ids, embed_table, latent_states, limits, cross_q, cross_kv, cross_o,
    attn_gain, self_qkv, self_o, mlp_gain, mlp_up, mlp_down,
):
    base, start, lanes = trig_tables()
    vmem = pl.BlockSpec(memory_space=pltpu.VMEM)
    dma = pltpu.SemaphoreType.DMA
    return pl.pallas_call(
        kernel,
        out_shape=jax.ShapeDtypeStruct((8, 1024), F32),
        in_specs=[pl.BlockSpec(memory_space=pltpu.HBM)] * 16,
        out_specs=vmem,
        scratch_shapes=[
            pltpu.VMEM((1, 1024), jnp.int32),
            pltpu.VMEM((8, 1024), BF16),
            pltpu.VMEM((1, 256), jnp.int32),
            pltpu.VMEM((1, 1024), F32),
            pltpu.VMEM((1, 1024), F32),
            pltpu.VMEM((64, 128), F32),
            pltpu.VMEM((8, 128), F32),
            pltpu.VMEM((1024, 1024), BF16),
            pltpu.VMEM((256, 1024), BF16),
            pltpu.VMEM((1024, 128), BF16),
            pltpu.VMEM((1024, 128), BF16),
            pltpu.VMEM((64, 1024), F32),
            pltpu.VMEM((1024, 1024), BF16),
            pltpu.VMEM((4, 1024, 128), BF16),
            pltpu.VMEM((4, 128, 1024), BF16),
            pltpu.VMEM((256, 128), F32),
            pltpu.VMEM((256, 128), F32),
            pltpu.VMEM((8, 8, 128), F32),
            pltpu.VMEM((2, 16, 8, 128), F32),
            pltpu.VMEM((16, 1, 1024), jnp.int32),
            pltpu.VMEM((16, 512), BF16),
            pltpu.VMEM((8, 16, 512), BF16),
            pltpu.VMEM((128, 1024), BF16),
            pltpu.VMEM((12, 32, 1024), BF16),
            pltpu.VMEM((16, 2, 32, 1024), BF16),
            pltpu.VMEM((4, 64, 1024), BF16),
            pltpu.VMEM((4, 64, 1024), BF16),
            pltpu.VMEM((256, 128), F32),
            pltpu.VMEM((256, 128), F32),
            pltpu.VMEM((2, 128, 128), F32),
            pltpu.VMEM((128, 128), F32),
            pltpu.VMEM((2, 32, 128), BF16),
            pltpu.VMEM((16, 32, 128), BF16),
            pltpu.VMEM((64, 1024), BF16),
            pltpu.VMEM((64, 1024), F32),
            pltpu.VMEM((4, 64, 256), BF16),
            pltpu.VMEM((8, 64, 128), BF16),
            pltpu.VMEM((8, 8, 1024), F32),
            pltpu.VMEM((8, 16, 512), BF16),
            pltpu.VMEM((8, 16, 512), BF16),
            pltpu.VMEM((8, 8, 1024), F32),
            dma((17,)),
            dma((57,)),
            dma((12,)),
            dma((4,)),
            dma((4,)),
            dma((12,)),
            dma((4,)),
        ],
        compiler_params=pltpu.CompilerParams(
            collective_id=0, has_side_effects=True, vmem_limit_bytes=60 << 20
        ),
        name="ar_step",
    )(
        context_ids.reshape(1, -1), latent_states, limits.reshape(1, -1),
        attn_gain.reshape(1, -1), mlp_gain.reshape(1, -1), self_qkv.T, self_o.T,
        jnp.asarray(start), jnp.asarray(lanes), jnp.asarray(base),
        embed_table, cross_q, cross_kv, cross_o, mlp_up, mlp_down,
    )


def solution(mesh):
    placed = (
        P(("dp", "seq")),
        P(),
        P(("dp", "seq"), None),
        P("dp"),
        P(),
        P(),
        P(),
        P(),
        P(None, "seq"),
        P(None, "seq"),
        P(),
        P(None, "seq"),
        P("seq", None),
    )
    return jax.shard_map(
        on_device, mesh=mesh, in_specs=placed, out_specs=P(("dp", "seq"), None), check_vma=False
    )
```

```python
import math

import jax
import jax.numpy as jnp
import numpy as np
from jax import lax
from jax.experimental import pallas as pl
from jax.experimental.pallas import tpu as pltpu
from jax.sharding import PartitionSpec as P

F32 = jnp.float32
BF16 = jnp.bfloat16
MESH = pl.DeviceIdType.MESH
LOW = -1e30


def trig_tables():
    periods = np.array([int(4.0 * 16384.0 ** (f / 31)) for f in range(32)], np.int64)

    def angles(positions):
        return 2.0 * np.pi * (positions[None, :] % periods[:, None]) / periods[:, None]

    base = angles(np.arange(1024))
    base = np.concatenate([np.cos(base), np.sin(base)]).astype(np.float32)
    start = angles(np.arange(32) * 1024)
    start = np.concatenate([np.cos(start), np.sin(start)]).astype(np.float32)
    start = np.pad(start, ((0, 0), (0, 96)))
    by_lane = np.tile(periods, 4).astype(np.float64)
    lanes = np.zeros((8, 128), np.float32)
    lanes[0], lanes[1], lanes[2] = by_lane, 1.0 / by_lane, 2.0 * np.pi / by_lane
    return base, start, lanes


def dot(left, right):
    return lax.dot_general(left, right, (((1,), (0,)), ((), ())), preferred_element_type=F32)


def dot_nt(left, right):
    return lax.dot_general(left, right, (((1,), (1,)), ((), ())), preferred_element_type=F32)


def iota(shape, axis):
    return lax.broadcasted_iota(jnp.int32, shape, axis)


def rms_scale(states, gain):
    mean_sq = jnp.mean(states * states, axis=-1, keepdims=True)
    return states * lax.rsqrt(mean_sq + 1e-05) * gain


def kernel(
    ids_hbm, states_hbm, limits_hbm, attn_gain_hbm, mlp_gain_hbm, qkv_hbm, selfo_hbm, start_hbm, lanes_hbm,
    base_hbm, embed_hbm, crossq_hbm, crosskv_hbm, crosso_hbm, up_hbm, down_hbm,
    out_ref,
    ids_ref, states_ref, limits_ref, attn_gain, mlp_gain, start_ref, lanes_ref,
    crossq, embed, ck, cv, base, crosso, updown_up, updown_dn,
    lim_nat, lim_perm, qsrc, qbuf, ids_all, stpack, strecv, wt, wqkv, selfo,
    keys_at, values_at, acc, peak, packs, comb, mixsrc, mixrecv, mixf, lat, kvall, mix2all, atts, part, precv, whole,
    loc, ss, rs, rs_up, rs_dn, rs_w, rs_kv,
):
    me = lax.axis_index("seq")
    dp = lax.axis_index("dp")
    core = lax.rem(me, 2)
    chip = me // 2
    x = lax.rem(chip, 2)
    z = chip // 2
    quad = lax.rem(me, 4)
    sib = me + 1 - 2 * core
    across = me + 2 - 4 * x
    diagonal = sib + 2 - 4 * x
    dp_pair = dp + 1 - 2 * lax.rem(dp, 2)
    y = dp // 2
    carrier = lax.rem(z, 4) == y
    quad_x = quad + 2 - 4 * x

    offsets = [(dz, dx) for dz in (4, 3, 5, 2, 6, 1, 7, 0) for dx in (1, 0) if dz or dx]
    same_core = [2 * lax.rem(z + dz, 8) + lax.rem(x + dx, 2) for dz, dx in offsets]
    ring = [lax.rem(me + 4 * dz, 32) for dz in (4, 3, 5, 2, 6, 1, 7)]

    def remote(src, dst, send, recv, seq, part_of=None):
        where = {"seq": seq} if part_of is None else {"dp": part_of, "seq": seq}
        return pltpu.make_async_remote_copy(
            src_ref=src, dst_ref=dst, send_sem=send, recv_sem=recv, device_id=where, device_id_type=MESH
        )

    def over(targets, body):
        for target in targets:
            body(target)

    barrier = pltpu.get_barrier_semaphore()

    def greet(seq, part_of=None):
        where = {"seq": seq} if part_of is None else {"dp": part_of, "seq": seq}
        pl.semaphore_signal(barrier, inc=1, device_id=where, device_id_type=MESH)

    over(same_core, lambda k: greet(2 * k + core))
    greet(sib)
    greet(diagonal)
    greet(across, dp_pair)
    over((1, 2, 3), lambda i: greet(me, lax.rem(dp + 2 * i, 8)))

    columns = pl.multiple_of(128 * z, 128)
    local = [
        pltpu.make_async_copy(crossq_hbm, crossq, loc.at[0]),
        pltpu.make_async_copy(embed_hbm, embed, loc.at[1]),
        pltpu.make_async_copy(crosskv_hbm.at[:, pl.ds(columns, 128)], ck, loc.at[2]),
        pltpu.make_async_copy(crosskv_hbm.at[:, pl.ds(columns + 1024, 128)], cv, loc.at[3]),
        pltpu.make_async_copy(base_hbm, base, loc.at[4]),
        pltpu.make_async_copy(up_hbm, updown_up.at[quad], loc.at[5]),
        pltpu.make_async_copy(down_hbm, updown_dn.at[quad], loc.at[6]),
        pltpu.make_async_copy(crosso_hbm, crosso, loc.at[7]),
        pltpu.make_async_copy(ids_hbm, ids_ref, loc.at[8]),
        pltpu.make_async_copy(states_hbm, states_ref, loc.at[9]),
        pltpu.make_async_copy(limits_hbm, limits_ref, loc.at[10]),
        pltpu.make_async_copy(attn_gain_hbm, attn_gain, loc.at[11]),
        pltpu.make_async_copy(mlp_gain_hbm, mlp_gain, loc.at[12]),
        pltpu.make_async_copy(start_hbm, start_ref, loc.at[13]),
        pltpu.make_async_copy(lanes_hbm, lanes_ref, loc.at[14]),
        pltpu.make_async_copy(qkv_hbm, wt.at[pl.ds(0, 96)], loc.at[15]),
        pltpu.make_async_copy(selfo_hbm, wt.at[pl.ds(96, 32)], loc.at[16]),
    ]
    for copy in local:
        copy.start()

    for n in (10, 9, 8, 14):
        local[n].wait()

    lim_nat[...] = jnp.broadcast_to(limits_ref[...].astype(F32), (128, 256)).T
    for c_of in range(2):
        for x_of in range(2):
            for z_of in range(8):
                slot = ((c_of * 2 + x_of) * 8 + z_of) * 8
                row = (z_of * 4 + x_of * 2 + c_of) * 8
                lim_perm[slot : slot + 8, :] = lim_nat[row : row + 8, :]

    local[0].wait()
    raw = dot(states_ref[...], crossq[...])
    period, inverse, factor = lanes_ref[0:1, :], lanes_ref[1:2, :], lanes_ref[2:3, :]
    position = lim_nat[pl.ds(pl.multiple_of(8 * me, 8), 8), :] - 1.0
    phase = position - jnp.floor(position * inverse) * period
    phase = jnp.where(phase < 0.0, phase + period, phase)
    phase = jnp.where(phase >= period, phase - period, phase) * factor
    lane8 = iota((8, 128), 1)
    first = lax.rem(lane8, 64) < 32
    cosines = jnp.cos(phase)
    sines = jnp.sin(phase)
    sines = jnp.where(first, -sines, sines)
    for p in range(8):
        tile = raw[:, 128 * p : 128 * p + 128]
        swapped = jnp.where(first, pltpu.roll(tile, 96, 1), pltpu.roll(tile, 32, 1))
        qsrc[p] = (tile * cosines + swapped * sines).astype(BF16).astype(F32) * 0.125
    qbuf[core, x * 8 + z] = qsrc[z]
    ids_all[chip] = ids_ref[...]
    packed = states_ref[...].astype(F32)
    packed = jnp.concatenate([packed[:, :512], packed[:, 512:]], axis=0).astype(BF16)
    stpack[...] = packed
    strecv[z] = packed

    pl.semaphore_wait(barrier, 21)

    def send_ids(k):
        remote(ids_ref, ids_all.at[chip], ss.at[0], rs.at[0], 2 * k + core).start()

    def send_queries(k):
        remote(qsrc.at[k // 2], qbuf.at[core, x * 8 + z], ss.at[1], rs.at[1], 2 * k + core).start()

    over(same_core, send_ids)
    over(same_core, send_queries)

    over(ring, lambda seq: remote(stpack, strecv.at[z], ss.at[2], rs.at[2], seq).start())
    local[16].wait()

    def send_selfo(seq):
        remote(wt.at[pl.ds(96, 32)], selfo.at[chip, core], ss.at[13], rs.at[3], seq).start()

    @pl.when(carrier)
    def _():
        selfo[chip, core] = wt[96:128, :]
        over(ring, send_selfo)

    local[15].wait()

    def unit_copies(i):
        unit = 3 * me + i
        index = 4 * (unit // 32) + lax.rem(unit, 4)
        target = 4 * (lax.rem(unit, 32) // 4) + quad
        away = remote(wt.at[pl.ds(32 * i, 32)], wqkv.at[index], ss.at[7 + i], rs_w.at[index], target)
        here = pltpu.make_async_copy(wt.at[pl.ds(32 * i, 32)], wqkv.at[index], rs_w.at[index])
        return target, away, here

    for i in range(3):
        target, away, here = unit_copies(i)
        pl.when(target != me)(away.start)
        pl.when(target == me)(here.start)

    own_up = [
        remote(up_hbm, updown_up.at[quad], ss.at[3], rs_up.at[quad], sib),
        remote(down_hbm, updown_dn.at[quad], ss.at[4], rs_dn.at[quad], sib),
        remote(up_hbm, updown_up.at[quad], ss.at[5], rs_up.at[quad], across, dp_pair),
        remote(down_hbm, updown_dn.at[quad], ss.at[6], rs_dn.at[quad], across, dp_pair),
    ]
    for copy in own_up:
        copy.start()

    local[1].wait()
    local[2].wait()
    local[3].wait()
    local[4].wait()
    local[13].wait()
    key_rows = dot(embed[...], ck[...]).T
    key_rows = jnp.where(x == 0, key_rows[0:64], key_rows[64:128])
    value_rows = dot(embed[...], cv[...]).T
    value_rows = jnp.where(x == 0, value_rows[0:64], value_rows[64:128])
    key_top = key_rows.astype(BF16)
    key_rest = (key_rows - key_top.astype(F32)).astype(BF16)
    table = jnp.concatenate([key_top, key_rest, value_rows.astype(BF16)], axis=0)

    def wait_in(buf, sem):
        pltpu.make_async_copy(buf, buf, sem).wait()

    wait_in(ids_all.at[pl.ds(0, 15)], rs.at[0])
    def key_block(j, slot):
        block = 2 * j + core
        ids = jnp.broadcast_to(ids_all[j].astype(F32).astype(BF16), (256, 1024))
        onehot = jnp.where(iota((256, 1024), 0).astype(F32).astype(BF16) == ids, 1.0, 0.0).astype(BF16)
        rows = dot(table, onehot)
        keys = rows[0:64] + rows[64:128]
        here = jnp.where(iota((64, 128), 1) == block, start_ref[...], 0.0)
        here = jnp.sum(here, axis=1, keepdims=True)
        cos_a, sin_a, cos_b, sin_b = here[0:32], here[32:64], base[0:32, :], base[32:64, :]
        cos = cos_a * cos_b - sin_a * sin_b
        sin = sin_a * cos_b + cos_a * sin_b
        one, two = keys[0:32], keys[32:64]
        turned = jnp.concatenate([one * cos - two * sin, two * cos + one * sin], axis=0)
        keys_at[slot] = turned.astype(BF16)
        values_at[slot] = rows[128:192].astype(BF16)

    for slot in range(4):
        key_block(slot, slot)
    wait_in(qbuf.at[core, pl.ds(0, 15)], rs.at[1])
    forward_q = remote(qbuf.at[core], qbuf.at[core], ss.at[14], rs.at[4], sib)
    forward_q.start()
    wait_in(qbuf.at[1 - core], rs.at[4])
    lane256 = iota((256, 128), 1)
    queries = jnp.where(lane256 // 64 == x, qbuf[...].reshape(256, 128), 0.0).astype(BF16)
    acc[...] = jnp.zeros((256, 128), F32)
    peak[...] = jnp.full((256, 128), LOW, F32)

    def context_block(j, slot, masked):
        block = 2 * j + core
        turned = keys_at[slot]
        scores = dot(queries, jnp.concatenate([turned, turned], axis=0))
        if masked:
            place = (block * 1024 + iota((1, 1024), 1)).astype(F32)
            scores = jnp.where(place < lim_perm[:, 0:1], scores, LOW)
        top = jnp.max(scores, axis=1, keepdims=True)
        weights = jnp.exp(scores - top).astype(BF16)
        values = jnp.concatenate([values_at[slot], jnp.ones((64, 1024), BF16)], axis=0)
        terms = dot_nt(weights, values)
        old = peak[...]
        new = jnp.maximum(old, top)
        acc[...] = acc[...] * jnp.exp(old - new) + terms * jnp.exp(top - new)
        peak[...] = new

    @pl.loop(0, 8, step=4)
    def _(start):
        for slot in range(4):
            context_block(start + slot, slot, False)
            key_block(start + slot + 4, slot)

    @pl.loop(8, 12, step=4)
    def _(start):
        for slot in range(4):
            context_block(start + slot, slot, True)
            key_block(start + slot + 4, slot)

    @pl.when(carrier)
    def _():
        wait_in(selfo.at[pl.ds(0, 1), 0], rs.at[3])

    @pl.when(jnp.logical_not(carrier))
    def _():
        wait_in(selfo.at[pl.ds(0, 2), 0], rs.at[3])

    along_x = []
    for n in range(2):
        brought = selfo.at[2 * y + 8 * n + x, core]
        along_x.append(remote(brought, brought, ss.at[43 + n], rs.at[11], across, dp_pair))
    for copy in along_x:
        copy.start()

    def unit_quad(index):
        unit = 32 * (index // 4) + 4 * z + index % 4
        return lax.rem(unit // 3, 4)

    def unit_across(index):
        return remote(wqkv.at[index], wqkv.at[index], ss.at[45 + index], rs_w.at[index], across, dp_pair)

    def unit_forward(index):
        return remote(wqkv.at[index], wqkv.at[index], ss.at[18 + index], rs_w.at[index], sib)

    def turn_unit(index):
        wait_in(wqkv.at[index], rs_w.at[index])
        unit_across(index).start()
        unit_forward(index).start()

    for index in range(12):
        pl.when(unit_quad(index) == quad)(lambda index=index: turn_unit(index))

    @pl.loop(12, 16, step=4)
    def _(start):
        for slot in range(4):
            context_block(start + slot, slot, True)

    wait_in(selfo.at[pl.ds(0, 2), 0], rs.at[11])
    along_y = []
    for i in range(1, 4):
        for n in range(2):
            brought = selfo.at[pl.ds(2 * y + 8 * n, 2), core]
            sem = ss.at[37 + 2 * (i - 1) + n]
            along_y.append(remote(brought, brought, sem, rs.at[10], me, lax.rem(dp + 2 * i, 8)))
    for copy in along_y:
        copy.start()


    packs[...] = jnp.where(lane256 == 127, peak[...], acc[...]).reshape(2, 128, 128)
    swap = remote(packs.at[1 - core], comb, ss.at[15], rs.at[5], sib)
    swap.start()

    wait_in(updown_up.at[quad_x], rs_up.at[quad_x])
    wait_in(updown_dn.at[quad_x], rs_dn.at[quad_x])
    forwards = [
        remote(updown_up.at[quad_x], updown_up.at[quad_x], ss.at[16], rs_up.at[quad_x], sib),
        remote(updown_dn.at[quad_x], updown_dn.at[quad_x], ss.at[17], rs_dn.at[quad_x], sib),
    ]
    for copy in forwards:
        copy.start()

    wait_in(comb, rs.at[5])
    mine, theirs = packs[core], comb[...]
    peak_a, peak_b = mine[:, 127:128], theirs[:, 127:128]
    top = jnp.maximum(peak_a, peak_b)
    both = mine * jnp.exp(peak_a - top) + theirs * jnp.exp(peak_b - top)
    mixed = both / both[:, 64:65]
    lane32 = iota((32, 128), 1)
    for x_of in range(2):
        low, high = mixed[64 * x_of : 64 * x_of + 32], mixed[64 * x_of + 32 : 64 * x_of + 64]
        mixsrc[x_of] = jnp.where(lane32 < 64, low, pltpu.roll(high, 64, 1)).astype(BF16)
    mixrecv[chip] = mixsrc[x]

    def send_mix(k):
        remote(mixsrc.at[lax.rem(k, 2)], mixrecv.at[chip], ss.at[30], rs.at[6], 2 * k + core).start()

    over(same_core, send_mix)

    def pass_unit(index):
        wait_in(wqkv.at[index], rs_w.at[index])
        unit_forward(index).start()

    for index in range(12):
        pl.when(unit_quad(index) == quad_x)(lambda index=index: pass_unit(index))


    wait_in(strecv.at[pl.ds(0, 7)], rs.at[2])
    for z_of in range(8):
        rows = strecv[z_of].astype(F32)
        lat[8 * z_of : 8 * z_of + 8, :] = jnp.concatenate([rows[0:8], rows[8:16]], axis=1)
    for index in range(12):
        pl.when(lax.rem(unit_quad(index), 2) != core)(
            lambda index=index: wait_in(wqkv.at[index], rs_w.at[index])
        )
    local[7].wait()
    local[11].wait()
    local[12].wait()
    wait_in(mixrecv.at[pl.ds(0, 15)], rs.at[6])
    for p in range(8):
        even, odd = mixrecv[2 * p].astype(F32), mixrecv[2 * p + 1].astype(F32)
        above = jnp.where(lane32 < 64, even, pltpu.roll(odd, 64, 1))
        below = jnp.where(lane32 < 64, pltpu.roll(even, 64, 1), odd)
        mixf[:, 128 * p : 128 * p + 128] = jnp.concatenate([above, below], axis=0).astype(BF16)
    latents = lat[...] + dot(mixf[...], crosso[...])
    normed = rms_scale(latents, attn_gain[...]).astype(BF16)
    lat[...] = latents

    projected = dot_nt(normed, wqkv[...].reshape(384, 1024)).astype(BF16)
    kvall[quad] = projected[:, 128:384]
    kv_copies = [
        remote(kvall.at[quad], kvall.at[quad], ss.at[32 + n], rs_kv.at[quad], seq)
        for n, seq in enumerate((sib, across, diagonal))
    ]
    for copy in kv_copies:
        copy.start()
    wait_in(selfo.at[pl.ds(0, 12), 0], rs.at[10])
    forward_o = remote(selfo.at[:, core], selfo.at[:, core], ss.at[31], rs.at[7], sib)
    forward_o.start()

    for other in (1, 2, 3):
        slot = lax.rem(quad + other, 4)
        wait_in(kvall.at[slot], rs_kv.at[slot])
    lane64 = iota((64, 128), 1)
    keys = kvall[:, :, 0:128].reshape(256, 128)
    values = kvall[:, :, 128:256].reshape(256, 128)
    key_lane = iota((64, 256), 1)
    key_row = 32 * (lax.rem(key_lane, 64) // 8) + 8 * (key_lane // 64) + lax.rem(key_lane, 8)
    query_at = iota((64, 256), 0)
    query_row = 32 * (query_at // 8) + 8 * quad + lax.rem(query_at, 8)
    causal = key_row <= query_row
    heads = []
    for head in range(2):
        only = jnp.where(lane64 // 64 == head, projected[:, 0:128].astype(F32), 0.0).astype(BF16)
        scores = jnp.where(causal, dot_nt(only, keys) * 0.125, LOW)
        weights = jnp.exp(scores - jnp.max(scores, axis=1, keepdims=True))
        total = jnp.sum(weights, axis=1, keepdims=True)
        coarse = weights.astype(BF16)
        fine = (weights - coarse.astype(F32)).astype(BF16)
        heads.append((dot(coarse, values) + dot(fine, values)) / total)
    mix2all[z] = jnp.where(lane64 < 64, heads[0], heads[1]).astype(BF16)
    over(ring, lambda seq: remote(mix2all.at[z], mix2all.at[z], ss.at[35], rs.at[8], seq).start())
    wait_in(selfo.at[:, 1 - core], rs.at[7])
    wait_in(mix2all.at[pl.ds(0, 7)], rs.at[8])
    mix2 = jnp.concatenate([mix2all[k] for k in range(8)], axis=1)
    attended = lat[...] + dot_nt(mix2, selfo[...].reshape(1024, 1024))
    atts[...] = attended.reshape(8, 8, 1024)
    normed = rms_scale(attended, mlp_gain[...]).astype(BF16)

    local[5].wait()
    local[6].wait()
    for slot in (quad + 1 - 2 * core, quad_x + 1 - 2 * core):
        wait_in(updown_up.at[slot], rs_up.at[slot])
        wait_in(updown_dn.at[slot], rs_dn.at[slot])
    hidden = []
    for half in range(2):
        ups = jnp.concatenate([updown_up[2 * half], updown_up[2 * half + 1]], axis=1)
        hidden.append(jax.nn.gelu(dot(normed, ups), approximate=True).astype(BF16))
    hidden = jnp.concatenate(hidden, axis=1)
    terms = dot(hidden, updown_dn[...].reshape(512, 1024))
    for k in range(8):
        rows = terms[8 * k : 8 * k + 8]
        part[k] = jnp.concatenate([rows[:, :512], rows[:, 512:]], axis=0).astype(BF16)

    def send_part(seq):
        remote(part.at[seq // 4], precv.at[z], ss.at[36], rs.at[9], seq).start()

    over(ring, send_part)
    whole[...] = terms.reshape(8, 8, 1024)
    own = whole[z]
    precv[z] = jnp.zeros((16, 512), BF16)
    wait_in(precv.at[pl.ds(0, 7)], rs.at[9])
    summed = precv[0].astype(F32)
    for k in range(1, 8):
        summed = summed + precv[k].astype(F32)
    out_ref[...] = atts[z] + (own + jnp.concatenate([summed[:8], summed[8:]], axis=1))

    def wait_out(buf, sem):
        pltpu.make_async_copy(buf, buf, sem).wait()

    wait_out(ids_all.at[pl.ds(0, 15)], ss.at[0])
    wait_out(qbuf.at[0, pl.ds(0, 15)], ss.at[1])
    wait_out(strecv.at[pl.ds(0, 7)], ss.at[2])
    for copy in own_up + forwards + kv_copies + along_x + along_y + [forward_q, swap, forward_o]:
        copy.wait_send()
    for i in range(3):
        target, away, _ = unit_copies(i)
        pl.when(target != me)(away.wait_send)
    for index in range(12):
        pl.when(lax.rem(unit_quad(index), 2) == core)(
            lambda index=index: unit_forward(index).wait_send()
        )
        pl.when(unit_quad(index) == quad)(lambda index=index: unit_across(index).wait_send())

    @pl.when(carrier)
    def _():
        wait_out(selfo.at[pl.ds(0, 7), 0], ss.at[13])

    wait_out(mixrecv.at[pl.ds(0, 15)], ss.at[30])
    wait_out(mix2all.at[pl.ds(0, 7)], ss.at[35])
    wait_out(precv.at[pl.ds(0, 7)], ss.at[36])


def on_device(
    context_ids, embed_table, latent_states, limits, cross_q, cross_kv, cross_o,
    attn_gain, self_qkv, self_o, mlp_gain, mlp_up, mlp_down,
):
    base, start, lanes = trig_tables()
    vmem = pl.BlockSpec(memory_space=pltpu.VMEM)
    dma = pltpu.SemaphoreType.DMA
    return pl.pallas_call(
        kernel,
        out_shape=jax.ShapeDtypeStruct((8, 1024), F32),
        in_specs=[pl.BlockSpec(memory_space=pltpu.HBM)] * 16,
        out_specs=vmem,
        scratch_shapes=[
            pltpu.VMEM((1, 1024), jnp.int32),
            pltpu.VMEM((8, 1024), BF16),
            pltpu.VMEM((1, 256), jnp.int32),
            pltpu.VMEM((1, 1024), F32),
            pltpu.VMEM((1, 1024), F32),
            pltpu.VMEM((64, 128), F32),
            pltpu.VMEM((8, 128), F32),
            pltpu.VMEM((1024, 1024), BF16),
            pltpu.VMEM((256, 1024), BF16),
            pltpu.VMEM((1024, 128), BF16),
            pltpu.VMEM((1024, 128), BF16),
            pltpu.VMEM((64, 1024), F32),
            pltpu.VMEM((1024, 1024), BF16),
            pltpu.VMEM((4, 1024, 128), BF16),
            pltpu.VMEM((4, 128, 1024), BF16),
            pltpu.VMEM((256, 128), F32),
            pltpu.VMEM((256, 128), F32),
            pltpu.VMEM((8, 8, 128), F32),
            pltpu.VMEM((2, 16, 8, 128), F32),
            pltpu.VMEM((16, 1, 1024), jnp.int32),
            pltpu.VMEM((16, 512), BF16),
            pltpu.VMEM((8, 16, 512), BF16),
            pltpu.VMEM((128, 1024), BF16),
            pltpu.VMEM((12, 32, 1024), BF16),
            pltpu.VMEM((16, 2, 32, 1024), BF16),
            pltpu.VMEM((4, 64, 1024), BF16),
            pltpu.VMEM((4, 64, 1024), BF16),
            pltpu.VMEM((256, 128), F32),
            pltpu.VMEM((256, 128), F32),
            pltpu.VMEM((2, 128, 128), F32),
            pltpu.VMEM((128, 128), F32),
            pltpu.VMEM((2, 32, 128), BF16),
            pltpu.VMEM((16, 32, 128), BF16),
            pltpu.VMEM((64, 1024), BF16),
            pltpu.VMEM((64, 1024), F32),
            pltpu.VMEM((4, 64, 256), BF16),
            pltpu.VMEM((8, 64, 128), BF16),
            pltpu.VMEM((8, 8, 1024), F32),
            pltpu.VMEM((8, 16, 512), BF16),
            pltpu.VMEM((8, 16, 512), BF16),
            pltpu.VMEM((8, 8, 1024), F32),
            dma((17,)),
            dma((57,)),
            dma((12,)),
            dma((4,)),
            dma((4,)),
            dma((12,)),
            dma((4,)),
        ],
        compiler_params=pltpu.CompilerParams(
            collective_id=0, has_side_effects=True, vmem_limit_bytes=60 << 20
        ),
        name="ar_step",
    )(
        context_ids.reshape(1, -1), latent_states, limits.reshape(1, -1),
        attn_gain.reshape(1, -1), mlp_gain.reshape(1, -1), self_qkv.T, self_o.T,
        jnp.asarray(start), jnp.asarray(lanes), jnp.asarray(base),
        embed_table, cross_q, cross_kv, cross_o, mlp_up, mlp_down,
    )


def solution(mesh):
    placed = (
        P(("dp", "seq")),
        P(),
        P(("dp", "seq"), None),
        P("dp"),
        P(),
        P(),
        P(),
        P(),
        P(None, "seq"),
        P(None, "seq"),
        P(),
        P(None, "seq"),
        P("seq", None),
    )
    return jax.shard_map(
        on_device, mesh=mesh, in_specs=placed, out_specs=P(("dp", "seq"), None), check_vma=False
    )
```
